512 devices in a mesh: tiles: 128 (over z, x, core), far: 4 (over y).
Axes of the slice: x: 4, y: 4, z: 16, core: 2. Of those that a mesh axis runs over, the one named last changes fastest.
Arguments:
- panel_geometry: float32 [512, 6, 128], P('tiles'), may hold values from -1 to 1
- adjoint: bfloat16 [512, 16, 128], P('tiles', 'far'), may hold values from -6 to 6
- strengths: bfloat16 [512, 16, 128], P('tiles', 'far'), may hold values from -6 to 6
- pair_target: int32 [4096], P('tiles'), may hold values from 0 to 3
- pair_owner: int32 [4096, 1], P('tiles'), may hold values from 0 to 127; in each aligned block of 32 rows (0 to 31, 32 to 63, ...) at most 2 rows name the same one
- pair_source: int32 [4096], P('tiles'), may hold values from 0 to 3
- pair_order: int32 [4096], P('tiles'), may hold values from 1 to 3
- pair_count: int32 [128], P('tiles'), may hold values from 24 to 32, as said below
- corner_vertex: int32 [512, 4, 128], P('tiles'), may hold values from 0 to 65535, as said below
Outputs:
- vertex_grad: float32 [3, 65536], P(None, 'tiles')
The draws below stay inside these ranges and needn't reach their ends.
Inputs may be any that keep to these rules, and one draw needn't show every extreme that they name: `pair_owner`: in the 32 slots of one list no owner is named more than 2 times; some list names one owner exactly 2 times. `pair_count`: some list is full with 32 live pairs. `corner_vertex`: every corner of a panel on tiles index t is a vertex owned by index t, t - 1, t + 1 or t + 128 / 2 (cyclically; the last is the mirrored half of the airframe); vertex v is owned by index v // 512.
All inputs are finite; a program needn't handle non-finite values.
Results may differ from the reference program's by a relative error of at most 0.00035.
Values may be sent and summed in bfloat16 or wider, within the bound.
A program may use at most 128 MiB of HBM per device.

```python
import math
import jax
import jax.numpy as jnp
import numpy as np
from jax import lax

PB = 128
B_DEV = 4
PAIRS_DEV = 32
CH = 16
BLOCKS = 512
PAIRS = 4096
CAP = 2
VERTS = 65536
N_TILES = 128


def draw_pair_count(key, part):
    base = jax.random.randint(jax.random.fold_in(key, 11), (N_TILES,), 3 * PAIRS_DEV // 4, PAIRS_DEV + 1, dtype=jnp.int32)
    busiest = jax.random.permutation(jax.random.fold_in(key, 12), N_TILES)[:max(1, N_TILES // 16)]
    return base.at[busiest].set(jnp.int32(PAIRS_DEV))


def draw_corner_vertex(key, part):
    vertex_width = B_DEV * PB
    owners = jnp.arange(BLOCKS, dtype=jnp.int32) // B_DEV
    rolled = jax.random.randint(jax.random.fold_in(key, 21), (BLOCKS, 4, PB), 0, 20, dtype=jnp.int32)
    moved = jnp.where(rolled < 3, -1, jnp.where(rolled < 5, N_TILES // 2, jnp.where(rolled > 16, 1, 0))).astype(jnp.int32)
    holder = (owners[:, None, None] + moved + N_TILES) % N_TILES
    within = jax.random.randint(jax.random.fold_in(key, 22), (BLOCKS, 4, PB), 0, vertex_width, dtype=jnp.int32)
    return holder * vertex_width + within


def set_ends(result, key, low, top_value):
    place = [jax.random.randint(jax.random.fold_in(key, axis), (), 0, length) for axis, length in enumerate(result.shape)]
    longest = result.shape.index(max(result.shape))
    neighbour = place[:longest] + [(place[longest] + 1) % result.shape[longest]] + place[longest + 1:]
    return result.at[tuple(place)].set(low).at[tuple(neighbour)].set(top_value)


def steps_of(stream_key, dims, split, least, largest):
    loudness = 1.0
    for axis_at, parts in split:
        draws = jax.random.uniform(jax.random.fold_in(jax.random.fold_in(stream_key, 6), axis_at), (parts,), jnp.float32, least / len(split), largest / len(split))
        loudness = loudness * jnp.repeat(jnp.exp(draws), dims[axis_at] // parts).reshape((-1,) + (1,) * (len(dims) - 1 - axis_at))
    return loudness


def shared_out(own_key, own, number, rows, number_of, top, limit, lean):
    ranking = jax.random.permutation(own_key, number_of)
    crowded, usual = load_shares(number_of, rows * top, limit, lean, True), load_shares(number_of, rows * top, limit, lean, False)
    places = jnp.arange(number_of)

    def named(lengths, offset_by):
        used = int((lengths > 0).sum())
        fixed = max(1, used // 4)
        shifted = fixed + (places - fixed + offset_by * (used - fixed)) % max(1, number_of - fixed)
        return jnp.zeros((number_of,), jnp.int32).at[ranking[jnp.where(places < fixed, places, shifted)]].set(jnp.asarray(lengths, jnp.int32))

    lengths = jnp.where(number % 4 == 0, named(crowded, number // 4), named(usual, number - number // 4 - 1))
    mixed = jax.random.permutation(jax.random.fold_in(own, 3), number_of)
    giver, sink = mixed[0:number_of // 2 * 2:2], mixed[1:number_of // 2 * 2:2]
    room = jnp.minimum(lengths[giver] - 1, limit - lengths[sink]) // 2
    room = jnp.where((giver == ranking[0]) | (sink == ranking[0]) | (lengths[sink] == 0), 0, jnp.maximum(room, 0))
    shifted = jax.random.randint(jax.random.fold_in(own, 4), (number_of // 2,), 0, 1 << 20) % (room + 1)
    lengths = lengths.at[giver].add(-shifted).at[sink].add(shifted)
    labels = jnp.searchsorted(jnp.cumsum(lengths), jnp.arange(rows * top), side="right").astype(jnp.int32)
    grid = labels.reshape(top, rows).T
    grid = grid[jax.random.permutation(jax.random.fold_in(own, 1), rows)]
    offset_by = jax.random.randint(jax.random.fold_in(own, 2), (rows, 1), 0, top)
    return jnp.take_along_axis(grid, (jnp.arange(top)[None, :] + offset_by) % top, axis=1)


def load_shares(count, total, bound, skew, full):
    portions = [(1 << 20) // math.isqrt(standing ** skew) + 1 for standing in range(1, count + 1)]
    largest = bound if full else min(bound, max(-(-total // count), total * portions[0] // sum(portions)))
    least = 1 if total - largest >= count - 1 else 0
    holding, spare = [largest] + [least] * (count - 1), total - largest - least * (count - 1)
    while spare > 0:
        candidates = [i for i in range(1, count) if holding[i] < largest] or [i for i in range(1, count) if holding[i] < bound]
        pool, remaining = sum([portions[i] for i in candidates]), spare
        for i in candidates:
            addition = min(bound - holding[i], max(1, remaining * portions[i] // pool), spare)
            holding[i] = holding[i] + addition
            spare = spare - addition
    return np.array(holding)


def gaussian(key, shape, width, reach, cuts=(), kind=jnp.bfloat16):
    loudness = steps_of(key, shape, cuts, -0.22, 0.18) if cuts else 1.0
    values = jax.random.normal(key, shape, jnp.float32) * width * loudness
    return jnp.minimum(jnp.maximum(values, -reach), reach).astype(kind)


def setup_inputs(seed: int = 0) -> dict:
    streams_of = jax.random.split(jax.random.key(seed), 10)
    panel_geometry = jnp.clip(jax.random.uniform(streams_of[0], (BLOCKS, 6, PB), jnp.float32, -1.0, 1.0) * steps_of(streams_of[0], (BLOCKS, 6, PB), ((0, 128),), -0.4, 0.0), -1.0, 1.0)
    adjoint = gaussian(streams_of[1], (BLOCKS, CH, PB), 1.0, 6.0, ((0, 128), (1, 4)))
    strengths = gaussian(streams_of[2], (BLOCKS, CH, PB), 1.0, 6.0, ((0, 128), (1, 4)))
    pair_target = set_ends(jax.random.randint(streams_of[3], (PAIRS,), 0, B_DEV), jax.random.fold_in(streams_of[3], 1), 0, B_DEV - 1).astype(jnp.int32)
    pair_owner_keys = jax.random.split(jax.random.fold_in(streams_of[4], 1), PAIRS // PAIRS_DEV)
    pair_owner_turns = jax.random.permutation(jax.random.fold_in(streams_of[4], 3), PAIRS // PAIRS_DEV)
    pair_owner = jax.vmap(lambda own, number: shared_out(jax.random.fold_in(streams_of[4], 2), own, number, PAIRS_DEV, N_TILES, 1, CAP, 1))(pair_owner_keys, pair_owner_turns).reshape((PAIRS, 1))
    pair_source = set_ends(jax.random.randint(streams_of[5], (PAIRS,), 0, B_DEV), jax.random.fold_in(streams_of[5], 1), 0, B_DEV - 1).astype(jnp.int32)
    pair_order = set_ends(jax.random.randint(streams_of[6], (PAIRS,), 1, 4), jax.random.fold_in(streams_of[6], 1), 1, 3).astype(jnp.int32)
    pair_count = draw_pair_count(jax.random.fold_in(streams_of[9], 71), 0)
    corner_vertex = draw_corner_vertex(jax.random.fold_in(streams_of[9], 71), 0)
    return dict(panel_geometry=panel_geometry, adjoint=adjoint, strengths=strengths, pair_target=pair_target, pair_owner=pair_owner, pair_source=pair_source, pair_order=pair_order, pair_count=pair_count, corner_vertex=corner_vertex)


def quadrature(orders):
    first = (orders == 1)[:, None]
    second = (orders == 2)[:, None]
    root_half = 0.5773502691896258
    root_fifth = 0.7745966692414834
    nodes = jnp.where(first, jnp.array([0.0, 0.0, 0.0], dtype=jnp.float32), jnp.where(second, jnp.array([-root_half, root_half, 0.0], dtype=jnp.float32), jnp.array([0.0, -root_fifth, root_fifth], dtype=jnp.float32)))
    weights = jnp.where(first, jnp.array([1.0, 0.0, 0.0], dtype=jnp.float32), jnp.where(second, jnp.array([0.5, 0.5, 0.0], dtype=jnp.float32), jnp.array([4.0 / 9.0, 5.0 / 18.0, 5.0 / 18.0], dtype=jnp.float32)))
    return (nodes, weights)

def tile_terms(target_geom, target_adjoint, source_geom, source_strength, orders):
    panel_coupling = jnp.einsum('avk,avu->aku', target_adjoint.astype(jnp.float32), source_strength.astype(jnp.float32), precision=lax.Precision.HIGHEST)
    nodes, weights = quadrature(orders)
    centre = target_geom[:, 0:3]
    target_grad = jnp.zeros(centre.shape, jnp.float32)
    source_grad = jnp.zeros(centre.shape, jnp.float32)
    for gauss_node_index in range(3):
        points = source_geom[:, 0:3] + 0.25 * nodes[:, gauss_node_index, None, None] * source_geom[:, 3:6]
        spread = centre[:, :, :, None] - points[:, :, None, :]
        squared = lax.optimization_barrier(jnp.sum(spread * spread, axis=1)) + 0.0625
        factor = weights[:, gauss_node_index, None, None] * panel_coupling / (squared * jnp.sqrt(squared))
        pulled = spread * factor[:, None]
        target_grad = target_grad - lax.optimization_barrier(jnp.sum(pulled, axis=3))
        source_grad = source_grad + lax.optimization_barrier(jnp.sum(pulled, axis=2))
    return (target_grad * 0.0078125, source_grad * 0.0078125)

def reference(panel_geometry, adjoint, strengths, pair_target, pair_owner, pair_source, pair_order, pair_count, corner_vertex):
    total = pair_target.shape[0]
    pair_ids = jnp.arange(total, dtype=jnp.int32)
    list_ids = pair_ids // PAIRS_DEV
    targets = list_ids * B_DEV + pair_target
    sources = pair_owner[:, 0] * B_DEV + pair_source
    alive = (pair_ids % PAIRS_DEV < pair_count[list_ids]).astype(jnp.float32)
    group_rows = 32

    def accumulate(panel_grad, group_index):
        start_row = group_index * group_rows
        group_targets = lax.dynamic_slice_in_dim(targets, start_row, group_rows, 0)
        tile_source_rows = lax.dynamic_slice_in_dim(sources, start_row, group_rows, 0)
        group_orders = lax.dynamic_slice_in_dim(pair_order, start_row, group_rows, 0)
        group_alive = lax.dynamic_slice_in_dim(alive, start_row, group_rows, 0)[:, None, None]
        target_grad, source_grad = tile_terms(panel_geometry[group_targets], adjoint[group_targets], panel_geometry[tile_source_rows], strengths[tile_source_rows], group_orders)
        panel_grad = panel_grad.at[group_targets].add(target_grad * group_alive)
        panel_grad = panel_grad.at[tile_source_rows].add(source_grad * group_alive)
        return (panel_grad, None)
    start_grad = jnp.zeros((BLOCKS, 3, PB), jnp.float32)
    panel_grad, _ = lax.scan(accumulate, start_grad, jnp.arange(total // group_rows, dtype=jnp.int32))
    corner_values = jnp.broadcast_to(0.25 * panel_grad[:, :, None, :], (BLOCKS, 3, 4, PB))
    corner_values = corner_values.transpose(1, 0, 2, 3).reshape(3, -1)
    flat_ids = corner_vertex.reshape(-1)
    return jnp.zeros((3, VERTS), jnp.float32).at[:, flat_ids].add(corner_values)
```

```python
import functools

import jax
import jax.numpy as jnp
from jax import lax
from jax.experimental import pallas as pl
from jax.experimental.pallas import tpu as pltpu
from jax.sharding import PartitionSpec as P

SLAB = 8
FAR = 4
PB = 128
PAIRS_DEV = 32
MESH = pl.DeviceIdType.MESH
F32 = jnp.float32
BF16 = jnp.bfloat16

ROOT_HALF = 0.5773502691896258
ROOT_FIFTH = 0.7745966692414834
RULES = {
    1: ((0.0, 1.0),),
    2: ((-ROOT_HALF, 0.5), (ROOT_HALF, 0.5)),
    3: ((0.0, 4.0 / 9.0), (-ROOT_FIFTH, 5.0 / 18.0), (ROOT_FIFTH, 5.0 / 18.0)),
}


def place(slabs):
    t = lax.axis_index("tiles")
    y = lax.axis_index("far")
    z = t // SLAB
    return t, z, t - z * SLAB, y, z % FAR


def send(src, dst, send_sem, recv_sem, device):
    pltpu.make_async_remote_copy(
        src_ref=src,
        dst_ref=dst,
        send_sem=send_sem,
        recv_sem=recv_sem,
        device_id=device,
        device_id_type=MESH,
    ).start()


def wait(ref, sem):
    pltpu.make_async_copy(ref, ref, sem).wait()


def gather_kernel(
    slabs,
    geom_ref,
    adj_ref,
    str_ref,
    tgt_ref,
    own_ref,
    src_ref,
    ord_ref,
    cnt_ref,
    sgeom_ref,
    sstr_ref,
    tadj_ref,
    tinfo_ref,
    codes_ref,
    send_sems,
    recv_sems,
):
    t, z, s, y, home = place(slabs)
    outer = slabs // FAR
    mine = y == home
    barrier = pltpu.get_barrier_semaphore()

    def greet(device):
        pl.semaphore_signal(barrier, inc=1, device_id=device, device_id_type=MESH)

    for zz in range(outer):
        for dy in range(1, FAR):
            yy = (home + dy) % FAR
            greet(((zz * FAR + y) * SLAB + s, yy))
    for dz in range(1, outer):
        greet(((((z // FAR + dz) % outer) * FAR + y) * SLAB + s, home))

    @pl.when(jnp.logical_not(mine))
    def _():
        greet((((z // FAR) * FAR + y) * SLAB + s, home))

    for ds in range(SLAB):
        for dy in range(FAR):
            if ds or dy:
                greet((z * SLAB + (s + ds) % SLAB, (y + dy) % FAR))

    tinfo_ref[s] = jnp.zeros((4, 8, PB), F32)
    for comp in range(3):
        for block in range(4):
            tinfo_ref[s, block, comp : comp + 1, :] = geom_ref[comp, block : block + 1, :]
    for row, ref in enumerate((tgt_ref, own_ref, src_ref, ord_ref)):
        tinfo_ref[s, 0, 3 + row : 4 + row, 0:PAIRS_DEV] = ref[...].astype(F32)
    slot = lax.broadcasted_iota(jnp.int32, (1, PB), 1)
    tinfo_ref[s, 0, 7:8, :] = jnp.where(slot < cnt_ref[0], 1.0, 0.0).astype(F32)

    pl.semaphore_wait(barrier, slabs + SLAB * FAR - 1 - mine.astype(jnp.int32))

    def send_source(zt, k):
        send(
            str_ref,
            sstr_ref.at[(z // FAR) * FAR + y],
            send_sems.at[0],
            recv_sems.at[0],
            (zt * SLAB + s, home),
        )

    for dz in range(1, slabs):
        send_source((z + dz) % slabs, 0)
    for dk in range(1, outer):
        zt = ((z // FAR + dk) % outer) * FAR + y
        send(
            geom_ref,
            sgeom_ref.at[z // FAR],
            send_sems.at[1],
            recv_sems.at[1],
            (zt * SLAB + s, home),
        )

    @pl.when(jnp.logical_not(mine))
    def _():
        send_source(z, 0)
        send(
            geom_ref,
            sgeom_ref.at[z // FAR],
            send_sems.at[1],
            recv_sems.at[1],
            (((z // FAR) * FAR + y) * SLAB + s, home),
        )

    @pl.when(mine)
    def _():
        sstr_ref[(z // FAR) * FAR + y] = str_ref[...]
        sgeom_ref[z // FAR] = geom_ref[...]

    for ds in range(1, SLAB):
        send(
            tinfo_ref.at[s],
            tinfo_ref.at[s],
            send_sems.at[3],
            recv_sems.at[3],
            (z * SLAB + (s + ds) % SLAB, y),
        )
    for ds in range(SLAB):
        for dy in range(FAR):
            if ds or dy:
                send(
                    adj_ref,
                    tadj_ref.at[s * FAR + y],
                    send_sems.at[2],
                    recv_sems.at[2],
                    (z * SLAB + (s + ds) % SLAB, (y + dy) % FAR),
                )
    tadj_ref[s * FAR + y] = adj_ref[...]

    wait(tinfo_ref.at[pl.ds(0, SLAB - 1)], recv_sems.at[3])
    codes_ref[...] = jnp.zeros((8, PB), jnp.int32)
    for k in range(SLAB):
        rows = tinfo_ref[k, 0].astype(jnp.int32)
        target, owner, source, order, live = (rows[r : r + 1] for r in range(3, 8))
        oz = owner // SLAB
        match = (
            (owner - oz * SLAB == s) & (oz - (oz // FAR) * FAR == y) & (live > 0) & (slot < PAIRS_DEV)
        )
        code = ((k * 4 + target) * 16 + (oz // FAR) * 4 + source) * 4 + order
        codes_ref[k : k + 1, :] = jnp.where(match, code, 0)

    wait(tadj_ref.at[pl.ds(0, SLAB * FAR - 1)], recv_sems.at[2])

    @pl.when(mine)
    def _():
        wait(sstr_ref.at[pl.ds(0, slabs - 1)], recv_sems.at[0])
        wait(sstr_ref.at[pl.ds(0, slabs - 1)], send_sems.at[0])
        if outer > 1:
            wait(sgeom_ref.at[pl.ds(0, outer - 1)], recv_sems.at[1])
            wait(sgeom_ref.at[pl.ds(0, outer - 1)], send_sems.at[1])

    @pl.when(jnp.logical_not(mine))
    def _():
        wait(sstr_ref.at[pl.ds(0, slabs)], recv_sems.at[0])
        wait(sstr_ref.at[pl.ds(0, slabs)], send_sems.at[0])
        wait(sgeom_ref.at[pl.ds(0, outer)], recv_sems.at[1])
        wait(sgeom_ref.at[pl.ds(0, outer)], send_sems.at[1])

    wait(tadj_ref.at[pl.ds(0, SLAB * FAR - 1)], send_sems.at[2])
    wait(tinfo_ref.at[pl.ds(0, SLAB - 1)], send_sems.at[3])


def pairs_kernel(
    slabs,
    codes_ref,
    sgeom_ref,
    sstr_ref,
    tadj_ref,
    tinfo_ref,
    source_ref,
    target_ref,
    s16_ref,
    t16_ref,
    tacc_ref,
    list_ref,
):
    outer = slabs // FAR

    def compact(k, n):
        row = k // (PAIRS_DEV // 8)
        column = (k - row * (PAIRS_DEV // 8)) * 8
        for i in range(8):
            code = codes_ref[row, column + i]
            list_ref[n] = code
            n = n + jnp.minimum(code, 1)
        return n

    total = lax.fori_loop(0, SLAB * PAIRS_DEV // 8, compact, jnp.int32(0))

    for a in range(outer):
        for yy in range(FAR):
            values = sstr_ref[a * FAR + yy].astype(F32)
            for j in range(4):
                s16_ref[a * 4 + j, 4 * yy : 4 * yy + 4, :] = values[4 * j : 4 * j + 4]
    for a in range(SLAB):
        for yy in range(FAR):
            values = tadj_ref[a * FAR + yy].astype(F32)
            for j in range(4):
                t16_ref[a * 4 + j, 4 * yy : 4 * yy + 4, :] = values[4 * j : 4 * j + 4]
    source_ref[...] = jnp.zeros(source_ref.shape, F32)
    tacc_ref[...] = jnp.zeros((PB, PB), F32)
    lane = lax.broadcasted_iota(jnp.int32, (1, PB), 1)

    def one_pair(i, carry):
        code = list_ref[i]
        order = code & 3
        source = (code >> 2) & 15
        target = code >> 6
        stack = jnp.concatenate([t16_ref[target], tinfo_ref[target // 4, target & 3]], axis=0)
        columns = stack.T
        coupling = jnp.dot(
            columns[:, 0:16].astype(BF16), s16_ref[source].astype(BF16), preferred_element_type=F32
        )
        centre = [columns[:, 16 + c : 17 + c] for c in range(3)]
        outer_index = source // 4
        block = source & 3
        base = [sgeom_ref[outer_index, c, pl.ds(block, 1), :] for c in range(3)]
        half = [0.25 * sgeom_ref[outer_index, 3 + c, pl.ds(block, 1), :] for c in range(3)]

        for rule, nodes in RULES.items():

            @pl.when(order == rule)
            def _():
                pulled = [None] * 3
                for node, weight in nodes:
                    differ = [
                        centre[c] - (base[c] + node * half[c] if node else base[c]) for c in range(3)
                    ]
                    squared = (
                        differ[0] * differ[0] + differ[1] * differ[1] + (differ[2] * differ[2] + 0.0625)
                    )
                    root = lax.rsqrt(squared)
                    factor = coupling * (root * root * root)
                    if weight != 1.0:
                        factor = factor * weight
                    for c in range(3):
                        term = factor * differ[c]
                        pulled[c] = term if pulled[c] is None else pulled[c] + term
                gathered = tacc_ref[...]
                for c in range(3):
                    source_ref[source, c : c + 1, :] += jnp.sum(pulled[c], axis=0, keepdims=True)
                    gathered = gathered - jnp.where(
                        lane == target * 4 + c, jnp.sum(pulled[c], axis=1, keepdims=True), 0.0
                    )
                tacc_ref[...] = gathered

        return carry

    lax.fori_loop(0, total, one_pair, 0)
    turned = tacc_ref[...].T
    for k in range(SLAB * 4):
        target_ref[k] = turned[4 * k : 4 * k + 4]


def scatter_kernel(
    slabs,
    source_ref,
    target_ref,
    corner_ref,
    out_ref,
    rs_source,
    rs_target,
    parts,
    landed,
    send_sems,
    recv_sems,
):
    t, z, s, y, home = place(slabs)
    outer = slabs // FAR
    tiles = slabs * SLAB
    mine = y == home
    barrier = pltpu.get_barrier_semaphore()

    def greet(device):
        pl.semaphore_signal(barrier, inc=1, device_id=device, device_id_type=MESH)

    for dz in range(1, slabs):
        greet((((z + dz) % slabs) * SLAB + s, home))

    @pl.when(jnp.logical_not(mine))
    def _():
        greet((z * SLAB + s, home))

    for ds in range(SLAB):
        for dy in range(FAR):
            if ds or dy:
                greet((z * SLAB + (s + ds) % SLAB, (y + dy) % FAR))
    shifts = (0, 1, tiles - 1, tiles // 2)
    for o in range(4):
        for dy in range(FAR):
            if o or dy:
                greet(((t + tiles - shifts[o]) % tiles, (y + dy) % FAR))

    vertex = corner_ref[y]
    holder = vertex // (4 * PB)
    away = holder - t
    away = jnp.where(away < 0, away + tiles, away)
    group = jnp.where(
        away == 0, 0, jnp.where(away == 1, 1, jnp.where(away == tiles - 1, 2, 3))
    )
    within = vertex - holder * (4 * PB)
    high = within // PB
    key = group * 4 + high
    low = within - high * PB
    row = lax.broadcasted_iota(jnp.int32, (PB, PB), 0)
    picks = jnp.concatenate(
        [jnp.where(row == low[j : j + 1], 1.0, 0.0).astype(BF16) for j in range(4)], axis=1
    )

    pl.semaphore_wait(barrier, slabs - mine.astype(jnp.int32) + SLAB * FAR - 1 + 15)

    def send_source(a, j):
        send(
            source_ref.at[a * 4 + j],
            rs_source.at[z],
            send_sems.at[0],
            recv_sems.at[0],
            ((a * FAR + y) * SLAB + s, j),
        )

    for da in range(outer):
        a = (z // FAR + da) % outer
        for dj in range(FAR):
            if dj:
                send_source(a, (y + dj) % FAR)
            elif da:
                send_source(a, y)

    @pl.when(jnp.logical_not(mine))
    def _():
        send_source(z // FAR, y)

    @pl.when(mine)
    def _():
        rs_source[z] = source_ref[(z // FAR) * 4 + y]

    for ds in range(SLAB):
        for dy in range(FAR):
            if ds or dy:
                st, yt = (s + ds) % SLAB, (y + dy) % FAR
                send(
                    target_ref.at[st * 4 + yt],
                    rs_target.at[s * FAR + y],
                    send_sems.at[1],
                    recv_sems.at[1],
                    (z * SLAB + st, yt),
                )
    rs_target[s * FAR + y] = target_ref[s * 4 + y]
    wait(rs_target.at[pl.ds(0, SLAB * FAR - 1)], recv_sems.at[1])

    @pl.when(mine)
    def _():
        wait(rs_source.at[pl.ds(0, slabs - 1)], recv_sems.at[0])

    @pl.when(jnp.logical_not(mine))
    def _():
        wait(rs_source.at[pl.ds(0, slabs)], recv_sems.at[0])

    grad = jnp.sum(rs_target[...], axis=0) + jnp.sum(rs_source[...], axis=0)
    grad = grad * (0.25 * 0.0078125)
    grad = jnp.concatenate([grad, grad], axis=0)
    wide = jnp.concatenate([grad] * 8, axis=0)
    rowkey = lax.broadcasted_iota(jnp.int32, (64, PB), 0) // 4
    first = wide.astype(BF16).astype(F32)
    second = wide - first
    spread = jnp.concatenate(
        [
            jnp.concatenate(
                [jnp.where(rowkey == key[j : j + 1], part, 0.0).astype(BF16) for j in range(4)], axis=1
            )
            for part in (first, second)
        ],
        axis=0,
    )
    sums = lax.dot_general(spread, picks, (((1,), (1,)), ((), ())), preferred_element_type=F32)
    sums = sums[0:64] + sums[64:128]
    for o in range(4):
        parts[o] = sums[16 * o : 16 * o + 16]
    for o in range(4):
        for dy in range(FAR):
            if o or dy:
                send(
                    parts.at[o],
                    landed.at[o * FAR + dy],
                    send_sems.at[2],
                    recv_sems.at[2],
                    ((t + shifts[o]) % tiles, (y + dy) % FAR),
                )
    landed[0] = parts[0]
    wait(landed.at[pl.ds(1, 15)], recv_sems.at[2])
    result = jnp.sum(landed[...], axis=0)
    for k in range(4):
        out_ref[:, k * PB : (k + 1) * PB] = result[4 * k : 4 * k + 3]

    wait(rs_target.at[pl.ds(0, SLAB * FAR - 1)], send_sems.at[1])

    @pl.when(mine)
    def _():
        wait(rs_source.at[pl.ds(0, slabs - 1)], send_sems.at[0])

    @pl.when(jnp.logical_not(mine))
    def _():
        wait(rs_source.at[pl.ds(0, slabs)], send_sems.at[0])

    wait(landed.at[pl.ds(1, 15)], send_sems.at[2])


def vmem():
    return pl.BlockSpec(memory_space=pltpu.VMEM)


def smem():
    return pl.BlockSpec(memory_space=pltpu.SMEM)


def shape(dims, dtype=F32):
    return jax.ShapeDtypeStruct(dims, dtype)


def per_device(
    panel_geometry,
    adjoint,
    strengths,
    pair_target,
    pair_owner,
    pair_source,
    pair_order,
    pair_count,
    corner_vertex,
):
    slabs = lax.axis_size("tiles") // SLAB
    outer = slabs // FAR
    row = lambda values: values.reshape(1, PAIRS_DEV)
    sgeom, sstr, tadj, tinfo, codes = pl.pallas_call(
        functools.partial(gather_kernel, slabs),
        out_shape=(
            shape((outer, 6, 4, PB)),
            shape((slabs, 16, PB), BF16),
            shape((SLAB * FAR, 16, PB), BF16),
            shape((SLAB, 4, 8, PB)),
            shape((8, PB), jnp.int32),
        ),
        in_specs=[vmem()] * 7 + [smem()],
        out_specs=(vmem(),) * 5,
        scratch_shapes=[pltpu.SemaphoreType.DMA((4,)), pltpu.SemaphoreType.DMA((4,))],
        compiler_params=pltpu.CompilerParams(collective_id=0, has_side_effects=True),
        name="gather_blocks",
    )(
        panel_geometry.transpose(1, 0, 2),
        adjoint.reshape(16, PB),
        strengths.reshape(16, PB),
        row(pair_target),
        row(pair_owner),
        row(pair_source),
        row(pair_order),
        pair_count,
    )
    source_grad, target_grad = pl.pallas_call(
        functools.partial(pairs_kernel, slabs),
        out_shape=(shape((outer * 4, 4, PB)), shape((SLAB * 4, 4, PB))),
        in_specs=[smem()] + [vmem()] * 4,
        out_specs=(vmem(),) * 2,
        scratch_shapes=[
            pltpu.VMEM((outer * 4, 16, PB), F32),
            pltpu.VMEM((SLAB * 4, 16, PB), F32),
            pltpu.VMEM((PB, PB), F32),
            pltpu.SMEM((SLAB * PAIRS_DEV + 8,), jnp.int32),
        ],
        name="pair_tiles",
    )(codes, sgeom, sstr, tadj, tinfo)
    return pl.pallas_call(
        functools.partial(scatter_kernel, slabs),
        out_shape=shape((3, 4 * PB)),
        in_specs=[vmem()] * 3,
        out_specs=vmem(),
        scratch_shapes=[
            pltpu.VMEM((slabs, 4, PB), F32),
            pltpu.VMEM((SLAB * FAR, 4, PB), F32),
            pltpu.VMEM((4, 16, PB), F32),
            pltpu.VMEM((16, 16, PB), F32),
            pltpu.SemaphoreType.DMA((3,)),
            pltpu.SemaphoreType.DMA((3,)),
        ],
        compiler_params=pltpu.CompilerParams(collective_id=1, has_side_effects=True),
        name="return_and_scatter",
    )(source_grad, target_grad, corner_vertex)


def solution(mesh):
    placed = (
        P("tiles", None, None),
        P("tiles", "far", None),
        P("tiles", "far", None),
        P("tiles"),
        P("tiles", None),
        P("tiles"),
        P("tiles"),
        P("tiles"),
        P("tiles", None, None),
    )
    return jax.shard_map(
        per_device, mesh=mesh, in_specs=placed, out_specs=P(None, "tiles"), check_vma=False
    )
```

```python
import functools

import jax
import jax.numpy as jnp
from jax import lax
from jax.experimental import pallas as pl
from jax.experimental.pallas import tpu as pltpu
from jax.sharding import PartitionSpec as P

SLAB = 8
FAR = 4
PB = 128
PAIRS_DEV = 32
MESH = pl.DeviceIdType.MESH
F32 = jnp.float32
BF16 = jnp.bfloat16

ROOT_HALF = 0.5773502691896258
ROOT_FIFTH = 0.7745966692414834
RULES = {
    1: ((0.0, 1.0),),
    2: ((-ROOT_HALF, 0.5), (ROOT_HALF, 0.5)),
    3: ((0.0, 4.0 / 9.0), (-ROOT_FIFTH, 5.0 / 18.0), (ROOT_FIFTH, 5.0 / 18.0)),
}


def place(slabs):
    t = lax.axis_index("tiles")
    y = lax.axis_index("far")
    z = t // SLAB
    return t, z, t - z * SLAB, y, z % FAR


def send(src, dst, send_sem, recv_sem, device):
    pltpu.make_async_remote_copy(
        src_ref=src,
        dst_ref=dst,
        send_sem=send_sem,
        recv_sem=recv_sem,
        device_id=device,
        device_id_type=MESH,
    ).start()


def wait(ref, sem):
    pltpu.make_async_copy(ref, ref, sem).wait()


def gather_kernel(
    slabs,
    geom_ref,
    adj_ref,
    str_ref,
    tgt_ref,
    own_ref,
    src_ref,
    ord_ref,
    cnt_ref,
    sgeom_ref,
    sstr_ref,
    tadj_ref,
    tinfo_ref,
    codes_ref,
    send_sems,
    recv_sems,
):
    t, z, s, y, home = place(slabs)
    outer = slabs // FAR
    mine = y == home
    barrier = pltpu.get_barrier_semaphore()

    def greet(device):
        pl.semaphore_signal(barrier, inc=1, device_id=device, device_id_type=MESH)

    for zz in range(outer):
        for dy in range(1, FAR):
            yy = (home + dy) % FAR
            greet(((zz * FAR + y) * SLAB + s, yy))
    for dz in range(1, outer):
        greet(((((z // FAR + dz) % outer) * FAR + y) * SLAB + s, home))

    @pl.when(jnp.logical_not(mine))
    def _():
        greet((((z // FAR) * FAR + y) * SLAB + s, home))

    for ds in range(1, SLAB):
        greet((z * SLAB + (s + ds) % SLAB, y))
    for dy in range(1, FAR):
        greet((t, (y + dy) % FAR))

    tinfo_ref[s] = jnp.zeros((4, 8, PB), F32)
    for comp in range(3):
        for block in range(4):
            tinfo_ref[s, block, comp : comp + 1, :] = geom_ref[comp, block : block + 1, :]
    for row, ref in enumerate((tgt_ref, own_ref, src_ref, ord_ref)):
        tinfo_ref[s, 0, 3 + row : 4 + row, 0:PAIRS_DEV] = ref[...].astype(F32)
    slot = lax.broadcasted_iota(jnp.int32, (1, PB), 1)
    tinfo_ref[s, 0, 7:8, :] = jnp.where(slot < cnt_ref[0], 1.0, 0.0).astype(F32)

    pl.semaphore_wait(barrier, slabs - mine.astype(jnp.int32) + SLAB - 1 + FAR - 1)

    def send_source(zt, k):
        send(
            str_ref,
            sstr_ref.at[(z // FAR) * FAR + y],
            send_sems.at[0],
            recv_sems.at[0],
            (zt * SLAB + s, home),
        )

    for dz in range(1, slabs):
        send_source((z + dz) % slabs, 0)
    for dk in range(1, outer):
        zt = ((z // FAR + dk) % outer) * FAR + y
        send(
            geom_ref,
            sgeom_ref.at[z // FAR],
            send_sems.at[1],
            recv_sems.at[1],
            (zt * SLAB + s, home),
        )

    @pl.when(jnp.logical_not(mine))
    def _():
        send_source(z, 0)
        send(
            geom_ref,
            sgeom_ref.at[z // FAR],
            send_sems.at[1],
            recv_sems.at[1],
            (((z // FAR) * FAR + y) * SLAB + s, home),
        )

    @pl.when(mine)
    def _():
        sstr_ref[(z // FAR) * FAR + y] = str_ref[...]
        sgeom_ref[z // FAR] = geom_ref[...]

    for dy in range(1, FAR):
        send(
            adj_ref,
            tadj_ref.at[s, y],
            send_sems.at[2],
            recv_sems.at[2],
            (t, (y + dy) % FAR),
        )
    tadj_ref[s, y] = adj_ref[...]
    for ds in range(1, SLAB):
        send(
            tinfo_ref.at[s],
            tinfo_ref.at[s],
            send_sems.at[3],
            recv_sems.at[3],
            (z * SLAB + (s + ds) % SLAB, y),
        )
    wait(tadj_ref.at[s, pl.ds(0, FAR - 1)], recv_sems.at[2])
    for ds in range(1, SLAB):
        send(
            tadj_ref.at[s],
            tadj_ref.at[s],
            send_sems.at[4],
            recv_sems.at[4],
            (z * SLAB + (s + ds) % SLAB, y),
        )

    wait(tinfo_ref.at[pl.ds(0, SLAB - 1)], recv_sems.at[3])
    codes_ref[...] = jnp.zeros((8, PB), jnp.int32)
    for k in range(SLAB):
        rows = tinfo_ref[k, 0].astype(jnp.int32)
        target, owner, source, order, live = (rows[r : r + 1] for r in range(3, 8))
        oz = owner // SLAB
        match = (
            (owner - oz * SLAB == s) & (oz - (oz // FAR) * FAR == y) & (live > 0) & (slot < PAIRS_DEV)
        )
        code = ((k * 4 + target) * 16 + (oz // FAR) * 4 + source) * 4 + order
        codes_ref[k : k + 1, :] = jnp.where(match, code, 0)

    wait(tadj_ref.at[pl.ds(0, SLAB - 1)], recv_sems.at[4])

    @pl.when(mine)
    def _():
        wait(sstr_ref.at[pl.ds(0, slabs - 1)], recv_sems.at[0])
        wait(sstr_ref.at[pl.ds(0, slabs - 1)], send_sems.at[0])
        if outer > 1:
            wait(sgeom_ref.at[pl.ds(0, outer - 1)], recv_sems.at[1])
            wait(sgeom_ref.at[pl.ds(0, outer - 1)], send_sems.at[1])

    @pl.when(jnp.logical_not(mine))
    def _():
        wait(sstr_ref.at[pl.ds(0, slabs)], recv_sems.at[0])
        wait(sstr_ref.at[pl.ds(0, slabs)], send_sems.at[0])
        wait(sgeom_ref.at[pl.ds(0, outer)], recv_sems.at[1])
        wait(sgeom_ref.at[pl.ds(0, outer)], send_sems.at[1])

    wait(tadj_ref.at[s, pl.ds(0, FAR - 1)], send_sems.at[2])
    wait(tadj_ref.at[pl.ds(0, SLAB - 1)], send_sems.at[4])
    wait(tinfo_ref.at[pl.ds(0, SLAB - 1)], send_sems.at[3])


def pairs_kernel(
    slabs,
    codes_ref,
    sgeom_ref,
    sstr_ref,
    tadj_ref,
    tinfo_ref,
    source_ref,
    target_ref,
    s16_ref,
    t16_ref,
    tacc_ref,
    list_ref,
    codes,
    codes_sem,
):
    outer = slabs // FAR

    copy = pltpu.make_async_copy(codes_ref, codes, codes_sem)
    copy.start()

    for a in range(outer):
        for yy in range(FAR):
            values = sstr_ref[a * FAR + yy].astype(F32)
            for j in range(4):
                s16_ref[a * 4 + j, 4 * yy : 4 * yy + 4, :] = values[4 * j : 4 * j + 4]
    for a in range(SLAB):
        for yy in range(FAR):
            values = tadj_ref[a, yy].astype(F32)
            for j in range(4):
                t16_ref[a * 4 + j, 4 * yy : 4 * yy + 4, :] = values[4 * j : 4 * j + 4]
    source_ref[...] = jnp.zeros(source_ref.shape, F32)
    tacc_ref[...] = jnp.zeros((PB, PB), F32)
    lane = lax.broadcasted_iota(jnp.int32, (1, PB), 1)

    def compact(k, n):
        row = k // (PAIRS_DEV // 8)
        column = (k - row * (PAIRS_DEV // 8)) * 8
        for i in range(8):
            code = codes[row, column + i]
            list_ref[n] = code
            n = n + jnp.minimum(code, 1)
        return n

    copy.wait()
    total = lax.fori_loop(0, SLAB * PAIRS_DEV // 8, compact, jnp.int32(0))

    def one_pair(i, carry):
        code = list_ref[i]
        order = code & 3
        source = (code >> 2) & 15
        target = code >> 6
        stack = jnp.concatenate([t16_ref[target], tinfo_ref[target // 4, target & 3]], axis=0)
        columns = stack.T
        coupling = jnp.dot(
            columns[:, 0:16].astype(BF16), s16_ref[source].astype(BF16), preferred_element_type=F32
        )
        centre = [columns[:, 16 + c : 17 + c] for c in range(3)]
        outer_index = source // 4
        block = source & 3
        base = [sgeom_ref[outer_index, c, pl.ds(block, 1), :] for c in range(3)]
        half = [0.25 * sgeom_ref[outer_index, 3 + c, pl.ds(block, 1), :] for c in range(3)]

        for rule, nodes in RULES.items():

            @pl.when(order == rule)
            def _():
                pulled = [None] * 3
                for node, weight in nodes:
                    differ = [
                        centre[c] - (base[c] + node * half[c] if node else base[c]) for c in range(3)
                    ]
                    squared = (
                        differ[0] * differ[0] + differ[1] * differ[1] + (differ[2] * differ[2] + 0.0625)
                    )
                    root = lax.rsqrt(squared)
                    factor = coupling * (root * root * root)
                    if weight != 1.0:
                        factor = factor * weight
                    for c in range(3):
                        term = factor * differ[c]
                        pulled[c] = term if pulled[c] is None else pulled[c] + term
                gathered = tacc_ref[...]
                for c in range(3):
                    source_ref[outer_index, c, pl.ds(block, 1), :] += jnp.sum(
                        pulled[c], axis=0, keepdims=True
                    )
                    gathered = gathered - jnp.where(
                        lane == (target // 4) * 16 + c * 4 + (target & 3), jnp.sum(pulled[c], axis=1, keepdims=True), 0.0
                    )
                tacc_ref[...] = gathered

        return carry

    lax.fori_loop(0, total, one_pair, 0)
    turned = tacc_ref[...].T
    for k in range(SLAB):
        for c in range(3):
            target_ref[k, c] = turned[16 * k + 4 * c : 16 * k + 4 * c + 4]


def scatter_kernel(
    slabs,
    source_ref,
    target_ref,
    corner_ref,
    out_ref,
    rs_source,
    rs_target,
    parts,
    landed,
    send_sems,
    recv_sems,
):
    t, z, s, y, home = place(slabs)
    outer = slabs // FAR
    tiles = slabs * SLAB
    mine = y == home
    base = (z // FAR) * FAR + y
    barrier = pltpu.get_barrier_semaphore()

    def greet(device):
        pl.semaphore_signal(barrier, inc=1, device_id=device, device_id_type=MESH)

    shifts = (0, 1, tiles - 1, tiles // 2)
    for o in (3, 1, 2, 0):
        for dy in range(FAR):
            if o or dy:
                greet(((t + tiles - shifts[o]) % tiles, (y + dy) % FAR))
    for da in range(1, outer):
        greet((((z // FAR + da) % outer * FAR + y) * SLAB + s, home))

    @pl.when(jnp.logical_not(mine))
    def _():
        greet((base * SLAB + s, home))

    for ds in range(1, SLAB):
        greet((z * SLAB + (s + ds) % SLAB, y))

    row = lax.broadcasted_iota(jnp.int32, (PB, PB), 0)
    picks = []
    keys = []
    for block in range(4):
        vertex = corner_ref[block]
        holder = vertex // (4 * PB)
        away = holder - t
        away = jnp.where(away < 0, away + tiles, away)
        group = jnp.where(
            away == 0, 0, jnp.where(away == 1, 1, jnp.where(away == tiles - 1, 2, 3))
        )
        within = vertex - holder * (4 * PB)
        high = within // PB
        low = within - high * PB
        keys.append(group * 4 + high)
        picks += [jnp.where(row == low[j : j + 1], 1.0, 0.0).astype(BF16) for j in range(4)]
    picks = jnp.concatenate(picks, axis=1)

    pl.semaphore_wait(barrier, 15 + outer - mine.astype(jnp.int32) + SLAB - 1)

    def send_source(a):
        send(
            source_ref.at[a],
            rs_source.at[z // FAR],
            send_sems.at[0],
            recv_sems.at[0],
            ((a * FAR + y) * SLAB + s, home),
        )

    for da in range(1, outer):
        send_source((z // FAR + da) % outer)

    @pl.when(jnp.logical_not(mine))
    def _():
        send_source(z // FAR)

    @pl.when(mine)
    def _():
        rs_source[z // FAR] = source_ref[z // FAR]

    for ds in range(1, SLAB):
        st = (s + ds) % SLAB
        send(
            target_ref.at[st],
            rs_target.at[s],
            send_sems.at[1],
            recv_sems.at[1],
            (z * SLAB + st, y),
        )
    rs_target[s] = target_ref[s]
    wait(rs_target.at[pl.ds(0, SLAB - 1)], recv_sems.at[1])

    @pl.when(mine)
    def _():
        if outer > 1:
            wait(rs_source.at[pl.ds(0, outer - 1)], recv_sems.at[0])

    @pl.when(jnp.logical_not(mine))
    def _():
        wait(rs_source.at[pl.ds(0, outer)], recv_sems.at[0])

    grad = jnp.sum(rs_target[...], axis=0) + jnp.sum(rs_source[...], axis=0)
    grad = grad * (0.25 * 0.0078125)
    rowkey = lax.broadcasted_iota(jnp.int32, (16, PB), 0)
    upper = [[], [], []]
    lower = [[], [], []]
    for block in range(4):
        for c in range(3):
            wide = jnp.broadcast_to(grad[c, block : block + 1], (16, PB))
            first = wide.astype(BF16)
            second = (wide - first.astype(F32)).astype(BF16)
            for j in range(4):
                here = rowkey == keys[block][j : j + 1]
                upper[c].append(jnp.where(here, first, jnp.zeros_like(first)))
                lower[c].append(jnp.where(here, second, jnp.zeros_like(second)))
    spread = jnp.concatenate([jnp.concatenate(part, axis=1) for part in upper + lower], axis=0)
    sums = lax.dot_general(spread, picks, (((1,), (1,)), ((), ())), preferred_element_type=F32)
    sums = sums[0:48] + sums[48:96]
    for o in range(4):
        for c in range(3):
            parts[o, c] = sums[16 * c + 4 * o : 16 * c + 4 * o + 4]
    for o in (3, 1, 2, 0):
        for dy in range(FAR):
            if o or dy:
                send(
                    parts.at[o],
                    landed.at[o * FAR + dy],
                    send_sems.at[2],
                    recv_sems.at[2],
                    ((t + shifts[o]) % tiles, (y + dy) % FAR),
                )
    landed[0] = parts[0]
    wait(landed.at[pl.ds(1, 15)], recv_sems.at[2])
    result = jnp.sum(landed[...], axis=0)
    for k in range(4):
        for c in range(3):
            out_ref[c : c + 1, k * PB : (k + 1) * PB] = result[c, k : k + 1]

    wait(rs_target.at[pl.ds(0, SLAB - 1)], send_sems.at[1])

    @pl.when(mine)
    def _():
        if outer > 1:
            wait(rs_source.at[pl.ds(0, outer - 1)], send_sems.at[0])

    @pl.when(jnp.logical_not(mine))
    def _():
        wait(rs_source.at[pl.ds(0, outer)], send_sems.at[0])

    wait(landed.at[pl.ds(1, 15)], send_sems.at[2])


def vmem():
    return pl.BlockSpec(memory_space=pltpu.VMEM)


def resident(dims, dtype):
    return pltpu.VMEM(dims, dtype)


def held(*arrays):
    return [pltpu.with_memory_space_constraint(a, pltpu.VMEM) for a in arrays]


def smem():
    return pl.BlockSpec(memory_space=pltpu.SMEM)


def shape(dims, dtype=F32):
    return jax.ShapeDtypeStruct(dims, dtype)


def per_device(
    panel_geometry,
    adjoint,
    strengths,
    pair_target,
    pair_owner,
    pair_source,
    pair_order,
    pair_count,
    corner_vertex,
):
    slabs = lax.axis_size("tiles") // SLAB
    outer = slabs // FAR
    row = lambda values: values.reshape(1, PAIRS_DEV)
    sgeom, sstr, tadj, tinfo, codes = pl.pallas_call(
        functools.partial(gather_kernel, slabs),
        out_shape=(
            resident((outer, 6, 4, PB), F32),
            resident((slabs, 16, PB), BF16),
            resident((SLAB, FAR, 16, PB), BF16),
            resident((SLAB, 4, 8, PB), F32),
            resident((8, PB), jnp.int32),
        ),
        in_specs=[vmem()] * 7 + [smem()],
        out_specs=(vmem(),) * 5,
        scratch_shapes=[pltpu.SemaphoreType.DMA((5,)), pltpu.SemaphoreType.DMA((5,))],
        compiler_params=pltpu.CompilerParams(collective_id=0, has_side_effects=True),
        name="gather_blocks",
    )(
        panel_geometry.transpose(1, 0, 2),
        adjoint.reshape(16, PB),
        strengths.reshape(16, PB),
        row(pair_target),
        row(pair_owner),
        row(pair_source),
        row(pair_order),
        pair_count,
    )
    source_grad, target_grad = pl.pallas_call(
        functools.partial(pairs_kernel, slabs),
        out_shape=(resident((outer, 3, 4, PB), F32), resident((SLAB, 3, 4, PB), F32)),
        in_specs=[vmem()] * 5,
        out_specs=(vmem(),) * 2,
        scratch_shapes=[
            pltpu.VMEM((outer * 4, 16, PB), F32),
            pltpu.VMEM((SLAB * 4, 16, PB), F32),
            pltpu.VMEM((PB, PB), F32),
            pltpu.SMEM((SLAB * PAIRS_DEV + 8,), jnp.int32),
            pltpu.SMEM((8, PB), jnp.int32),
            pltpu.SemaphoreType.DMA,
        ],
        name="pair_tiles",
    )(*held(codes, sgeom, sstr, tadj, tinfo))
    return pl.pallas_call(
        functools.partial(scatter_kernel, slabs),
        out_shape=shape((3, 4 * PB)),
        in_specs=[vmem()] * 3,
        out_specs=vmem(),
        scratch_shapes=[
            pltpu.VMEM((outer, 3, 4, PB), F32),
            pltpu.VMEM((SLAB, 3, 4, PB), F32),
            pltpu.VMEM((4, 3, 4, PB), F32),
            pltpu.VMEM((16, 3, 4, PB), F32),
            pltpu.SemaphoreType.DMA((3,)),
            pltpu.SemaphoreType.DMA((3,)),
        ],
        compiler_params=pltpu.CompilerParams(collective_id=1, has_side_effects=True),
        name="return_and_scatter",
    )(*held(source_grad, target_grad), corner_vertex)


def solution(mesh):
    placed = (
        P("tiles", None, None),
        P("tiles", "far", None),
        P("tiles", "far", None),
        P("tiles"),
        P("tiles", None),
        P("tiles"),
        P("tiles"),
        P("tiles"),
        P("tiles", None, None),
    )
    return jax.shard_map(
        per_device, mesh=mesh, in_specs=placed, out_specs=P(None, "tiles"), check_vma=False
    )
```

```python
import functools

import jax
import jax.numpy as jnp
from jax import lax
from jax.experimental import pallas as pl
from jax.experimental.pallas import tpu as pltpu
from jax.sharding import PartitionSpec as P

SLAB = 8
FAR = 4
PB = 128
PAIRS_DEV = 32
MESH = pl.DeviceIdType.MESH
F32 = jnp.float32
BF16 = jnp.bfloat16

ROOT_HALF = 0.5773502691896258
ROOT_FIFTH = 0.7745966692414834
WITHIN = 4 * PB
def place(slabs):
    t = lax.axis_index("tiles")
    y = lax.axis_index("far")
    z = t // SLAB
    return t, z, t - z * SLAB, y, z % FAR


def send(src, dst, send_sem, recv_sem, device):
    pltpu.make_async_remote_copy(
        src_ref=src,
        dst_ref=dst,
        send_sem=send_sem,
        recv_sem=recv_sem,
        device_id=device,
        device_id_type=MESH,
    ).start()


def wait(ref, sem):
    pltpu.make_async_copy(ref, ref, sem).wait()


def split(values):
    high = values.astype(BF16).astype(F32)
    rest = values - high
    middle = rest.astype(BF16).astype(F32)
    return high, middle, (rest - middle).astype(BF16).astype(F32)


def squares(points, offset):
    total = points[0:1] * points[0:1] + points[1:2] * points[1:2] + (points[2:3] * points[2:3] + offset)
    return split(total)


def kernel(
    slabs,
    geom_ref,
    adj_ref,
    str_ref,
    tgt_ref,
    own_ref,
    src_ref,
    ord_ref,
    cnt_ref,
    corner_ref,
    out_ref,
    sgeom,
    sstr,
    tadj,
    tinfo,
    left,
    trow,
    sbase,
    srow,
    right,
    right_far,
    source_acc,
    target_acc,
    rs_source,
    rs_target,
    parts,
    landed,
    codes_v,
    codes,
    codes_sem,
    str_sems,
    geom_sems,
    send_sems,
    recv_sems,
):
    t, z, s, y, home = place(slabs)
    outer = slabs // FAR
    quarter = z // FAR
    tiles = slabs * SLAB
    mine = y == home
    other = jnp.logical_not(mine)
    barrier = pltpu.get_barrier_semaphore()
    near_first = {1: (0,), 2: (0, 1), 4: (0, 1, 3, 2)}[outer]
    shifts = (0, 1, tiles - 1, tiles // 2)

    def greet(device):
        pl.semaphore_signal(barrier, inc=1, device_id=device, device_id_type=MESH)

    for zz in range(outer):
        for dy in range(1, FAR):
            greet(((zz * FAR + y) * SLAB + s, (home + dy) % FAR))
    for dz in range(1, outer):
        greet(((((quarter + dz) % outer) * FAR + y) * SLAB + s, home))

    @pl.when(other)
    def _():
        greet(((quarter * FAR + y) * SLAB + s, home))

    for o in (3, 1, 2, 0):
        for dy in range(FAR):
            if o or dy:
                greet(((t + tiles - shifts[o]) % tiles, (y + dy) % FAR))
    for ds in range(1, SLAB):
        greet((z * SLAB + (s + ds) % SLAB, y))

    lane = lax.broadcasted_iota(jnp.int32, (1, PB), 1)
    tinfo[s] = jnp.zeros((4, 8, PB), F32)
    for comp in range(3):
        for block in range(4):
            tinfo[s, block, comp : comp + 1, :] = geom_ref[comp, block : block + 1, :]
    live = lax.broadcasted_iota(jnp.int32, (1, PAIRS_DEV), 1) < cnt_ref[0]
    orders = jnp.where(live, ord_ref[...], 0)
    for row, values in enumerate((tgt_ref[...], own_ref[...], src_ref[...], orders)):
        tinfo[s, 0, 4 + row : 5 + row, 0:PAIRS_DEV] = values.astype(F32)

    pl.semaphore_wait(barrier, slabs - mine.astype(jnp.int32) + SLAB - 1 + 15)

    def send_strengths(zt):
        da = (quarter - zt // FAR + outer) % outer
        send(str_ref, sstr.at[da, y], send_sems.at[0], str_sems.at[da], (zt * SLAB + s, home))

    def send_geometry(zt):
        da = (quarter - zt // FAR + outer) % outer
        send(geom_ref, sgeom.at[da], send_sems.at[1], geom_sems.at[da], (zt * SLAB + s, home))

    for step in range(slabs // 2, 0, -1):
        send_strengths((z + step) % slabs)
        if 2 * step != slabs:
            send_strengths((z + slabs - step) % slabs)
    for dk in near_first[::-1]:
        if dk:
            send_geometry(((quarter + dk) % outer) * FAR + y)

    @pl.when(other)
    def _():
        send_strengths(z)
        send_geometry(quarter * FAR + y)

    @pl.when(mine)
    def _():
        sstr[0, y] = str_ref[...]
        sgeom[0] = geom_ref[...]

    for dy in range(1, FAR):
        send(adj_ref, tadj.at[s, y], send_sems.at[2], recv_sems.at[2], (t, (y + dy) % FAR))
    for ds in range(1, SLAB):
        peer = (z * SLAB + (s + ds) % SLAB, y)
        send(tinfo.at[s], tinfo.at[s], send_sems.at[3], recv_sems.at[3], peer)
    tadj[s, y] = adj_ref[...]
    wait(tadj.at[s, pl.ds(0, FAR - 1)], recv_sems.at[2])
    for ds in range(1, SLAB):
        peer = (z * SLAB + (s + ds) % SLAB, y)
        send(tadj.at[s], tadj.at[s], send_sems.at[4], recv_sems.at[4], peer)

    row = lax.broadcasted_iota(jnp.int32, (PB, PB), 0)
    picks = []
    keys = []
    for block in range(4):
        vertex = corner_ref[block]
        holder = vertex // (4 * PB)
        away = holder - t
        away = jnp.where(away < 0, away + tiles, away)
        group = jnp.where(
            away == 0, 0, jnp.where(away == 1, 1, jnp.where(away == tiles - 1, 2, 3))
        )
        within = vertex - holder * (4 * PB)
        high = within // PB
        low = within - high * PB
        keys.append(group * 4 + high)
        picks += [jnp.where(row == low[j : j + 1], 1.0, 0.0).astype(BF16) for j in range(4)]
    picks = jnp.concatenate(picks, axis=1)

    wait(tinfo.at[pl.ds(0, SLAB - 1)], recv_sems.at[3])
    place_of = lax.broadcasted_iota(jnp.int32, (8, PB), 0)
    wide_lane = lax.broadcasted_iota(jnp.int32, (8, PB), 1)
    da_of = place_of // 2
    wanted = ((quarter + da_of) % outer * FAR + y) * SLAB + s
    before = jnp.where(
        lax.broadcasted_iota(jnp.int32, (PB, PB), 0) < lax.broadcasted_iota(jnp.int32, (PB, PB), 1), 1.0, 0.0
    ).astype(BF16)
    for k in range(SLAB):
        rows = tinfo[k, 0].astype(jnp.int32)
        target, owner, source, order = (rows[r : r + 1] for r in range(4, 8))
        match = (owner == wanted) & (order > 0) & (wide_lane < PAIRS_DEV) & (da_of < outer)
        count = jnp.dot(
            jnp.where(match, 1.0, 0.0).astype(BF16), before, preferred_element_type=F32
        ).astype(jnp.int32)
        code = (target * 4 + source) * 4 + order
        chosen = jnp.where(match & (count == place_of - 2 * da_of), code, 0).astype(F32)
        total = jnp.sum(chosen, axis=1, keepdims=True).astype(jnp.int32)
        codes_v[k] = jnp.broadcast_to(total, (8, PB))
    copy = pltpu.make_async_copy(codes_v, codes, codes_sem)
    copy.start()

    wait(tadj.at[pl.ds(0, SLAB - 1)], recv_sems.at[4])
    zero4 = jnp.zeros((4, PB), F32)
    one = jnp.ones((1, PB), F32)
    zero1 = jnp.zeros((1, PB), F32)

    def prepare_list(k, carry):
        conditions = [tadj[k, yy].astype(F32) for yy in range(FAR)]
        for block in range(4):
            centre = tinfo[k, block][0:4]
            high, middle, low = split(centre)
            sq = squares(centre, 0.0)
            stack = jnp.concatenate(
                [c[4 * block : 4 * block + 4] for c in conditions]
                + [high, high, high, middle, middle, low]
                + [*sq, one, one, one, zero1, zero1],
                axis=0,
            )
            left[k * 4 + block] = stack.T.astype(BF16)
            trow[k * 4 + block] = jnp.concatenate(
                [one, zero1, zero1, zero1, high, middle, low], axis=0
            ).astype(BF16)
        target_acc[k] = jnp.zeros((4, 4, PB), F32)
        return carry

    lax.fori_loop(0, SLAB, prepare_list, 0)
    copy.wait()

    for da in near_first:
        if da:
            wait(sstr.at[da], str_sems.at[da])
            wait(sgeom.at[da], geom_sems.at[da])
        else:

            @pl.when(mine)
            def _():
                wait(sstr.at[0, pl.ds(0, FAR - 1)], str_sems.at[0])

            @pl.when(other)
            def _():
                wait(sstr.at[0], str_sems.at[0])
                wait(sgeom.at[0], geom_sems.at[0])

        conditions = [sstr[da, yy].astype(F32) for yy in range(FAR)]
        for block in range(4):
            base = jnp.concatenate([sgeom[da, c, block : block + 1, :] for c in range(3)] + [zero1], axis=0)
            half = 0.25 * jnp.concatenate(
                [sgeom[da, 3 + c, block : block + 1, :] for c in range(3)] + [zero1], axis=0
            )
            sbase[block] = jnp.concatenate([base, half], axis=0)
            first, second = split(base), split(half)
            srow[block] = jnp.concatenate(
                [
                    jnp.concatenate([one, zero1, zero1, zero1, *first], axis=0),
                    jnp.concatenate([zero4, *second], axis=0),
                ],
                axis=1,
            ).astype(BF16)

            def distance(points):
                high, middle, low = (-2.0 * part for part in split(points))
                sq = squares(points, 0.0625)
                return jnp.concatenate(
                    [zero4] * 4
                    + [high, middle, low, high, middle, high]
                    + [one, one, one, *sq, zero1, zero1],
                    axis=0,
                )

            coupled = jnp.concatenate(
                [c[4 * block : 4 * block + 4] for c in conditions] + [zero4] * 8, axis=0
            )
            right[block] = jnp.concatenate([coupled, distance(base)], axis=1).astype(BF16)
            for rule, node in enumerate((ROOT_HALF, ROOT_FIFTH)):
                right_far[block * 2 + rule] = jnp.concatenate(
                    [distance(base + node * half), distance(base - node * half)], axis=1
                ).astype(BF16)
        source_acc[da] = jnp.zeros((4, 4, PB), F32)

        def one_list(k, carry, da=da):
            for occurrence in range(2):
                code = codes[k, 2 * da + occurrence, 0]
                order = code & 3
                source = (code >> 2) & 3
                target = (code >> 4) & 3
                centre_weight = jnp.where(order == 1, 1.0, jnp.where(order == 3, 4.0 / 9.0, 0.0))
                side_weight = jnp.where(order == 2, 0.5, jnp.where(order == 3, 5.0 / 18.0, 0.0))
                shift_weight = jnp.where(
                    order == 2, 0.5 * ROOT_HALF, jnp.where(order == 3, 5.0 / 18.0 * ROOT_FIFTH, 0.0)
                )
                columns = left[k * 4 + target]
                inner = jnp.dot(columns, right[source], preferred_element_type=F32)
                sides = jnp.dot(columns, right_far[source * 2 + ((order + 1) >> 2)], preferred_element_type=F32)
                roots = lax.rsqrt(inner[:, PB:])
                pulls = lax.rsqrt(sides)
                roots = roots * roots * roots
                pulls = pulls * pulls * pulls
                coupling = inner[:, :PB]
                plus, minus = pulls[:, :PB], pulls[:, PB:]
                both = coupling * (centre_weight * roots + side_weight * (plus + minus))
                skew = (shift_weight * coupling) * (plus - minus)
                high = jnp.concatenate([both.astype(BF16), skew.astype(BF16)], axis=1)
                low = jnp.concatenate(
                    [
                        (both - high[:, :PB].astype(F32)).astype(BF16),
                        (skew - high[:, PB:].astype(F32)).astype(BF16),
                    ],
                    axis=1,
                )
                rows = trow[k * 4 + target]
                by_source = jnp.dot(rows, high, preferred_element_type=F32) + jnp.dot(
                    rows, low, preferred_element_type=F32
                )
                lines = srow[source]
                across = (((1,), (1,)), ((), ()))
                by_target = lax.dot_general(
                    lines, high, across, preferred_element_type=F32
                ) + lax.dot_general(lines, low, across, preferred_element_type=F32)
                points = sbase[source]
                pulled = (
                    by_source[4:8, :PB]
                    + by_source[8:12, :PB]
                    + by_source[12:16, :PB]
                    - points[0:4] * by_source[0:1, :PB]
                    - points[4:8] * by_source[0:1, PB:]
                )
                pushed = (
                    by_target[4:8]
                    + by_target[8:12]
                    + by_target[12:16]
                    - tinfo[k, target][0:4] * by_target[0:1]
                )
                for block in range(4):
                    source_acc[da, block] += jnp.where(source == block, 1.0, 0.0) * pulled
                    target_acc[k, block] += jnp.where(target == block, 1.0, 0.0) * pushed
            return carry

        lax.fori_loop(0, SLAB, one_list, 0)

        def send_source(da=da):
            send(
                source_acc.at[da],
                rs_source.at[quarter],
                send_sems.at[5],
                recv_sems.at[5],
                ((((quarter + da) % outer) * FAR + y) * SLAB + s, home),
            )

        if da:
            send_source()
        else:
            pl.when(other)(send_source)

            @pl.when(mine)
            def _():
                rs_source[quarter] = source_acc[0]

    for ds in range(1, SLAB):
        st = (s + ds) % SLAB
        send(target_acc.at[st], rs_target.at[s], send_sems.at[6], recv_sems.at[6], (z * SLAB + st, y))
    rs_target[s] = target_acc[s]
    wait(rs_target.at[pl.ds(0, SLAB - 1)], recv_sems.at[6])

    @pl.when(mine)
    def _():
        if outer > 1:
            wait(rs_source.at[pl.ds(0, outer - 1)], recv_sems.at[5])

    @pl.when(other)
    def _():
        wait(rs_source.at[pl.ds(0, outer)], recv_sems.at[5])

    grad = jnp.sum(rs_target[...], axis=0) + jnp.sum(rs_source[...], axis=0)
    grad = grad * (0.25 * 0.0078125)
    rowkey = lax.broadcasted_iota(jnp.int32, (16, PB), 0)
    upper = [[], [], []]
    lower = [[], [], []]
    for block in range(4):
        for c in range(3):
            wide = jnp.broadcast_to(grad[block, c : c + 1], (16, PB))
            first = wide.astype(BF16)
            second = (wide - first.astype(F32)).astype(BF16)
            for j in range(4):
                here = rowkey == keys[block][j : j + 1]
                upper[c].append(jnp.where(here, first, jnp.zeros_like(first)))
                lower[c].append(jnp.where(here, second, jnp.zeros_like(second)))
    spread = jnp.concatenate([jnp.concatenate(part, axis=1) for part in upper + lower], axis=0)
    sums = lax.dot_general(spread, picks, (((1,), (1,)), ((), ())), preferred_element_type=F32)
    sums = sums[0:48] + sums[48:96]
    for o in range(4):
        for c in range(3):
            parts[o, c] = sums[16 * c + 4 * o : 16 * c + 4 * o + 4]
    for o in (3, 1, 2, 0):
        for dy in range(FAR):
            if o or dy:
                send(
                    parts.at[o],
                    landed.at[o * FAR + dy],
                    send_sems.at[7],
                    recv_sems.at[7],
                    ((t + shifts[o]) % tiles, (y + dy) % FAR),
                )
    landed[0] = parts[0]
    wait(landed.at[pl.ds(1, 15)], recv_sems.at[7])
    result = jnp.sum(landed[...], axis=0)
    for k in range(4):
        for c in range(3):
            out_ref[c : c + 1, k * PB : (k + 1) * PB] = result[c, k : k + 1]

    wait(tadj.at[s, pl.ds(0, FAR - 1)], send_sems.at[2])
    wait(tinfo.at[pl.ds(0, SLAB - 1)], send_sems.at[3])
    wait(tadj.at[pl.ds(0, SLAB - 1)], send_sems.at[4])
    wait(rs_target.at[pl.ds(0, SLAB - 1)], send_sems.at[6])
    wait(landed.at[pl.ds(1, 15)], send_sems.at[7])

    @pl.when(mine)
    def _():
        if outer > 1:
            wait(sstr.at[pl.ds(0, outer - 1)], send_sems.at[0])
            wait(sgeom.at[pl.ds(0, outer - 1)], send_sems.at[1])
            wait(rs_source.at[pl.ds(0, outer - 1)], send_sems.at[5])
        wait(sstr.at[0, pl.ds(0, FAR - 1)], send_sems.at[0])

    @pl.when(other)
    def _():
        wait(sstr, send_sems.at[0])
        wait(sgeom, send_sems.at[1])
        wait(rs_source, send_sems.at[5])


def vmem():
    return pl.BlockSpec(memory_space=pltpu.VMEM)


def smem():
    return pl.BlockSpec(memory_space=pltpu.SMEM)


def per_device(
    panel_geometry,
    adjoint,
    strengths,
    pair_target,
    pair_owner,
    pair_source,
    pair_order,
    pair_count,
    corner_vertex,
):
    slabs = lax.axis_size("tiles") // SLAB
    outer = slabs // FAR
    row = lambda values: values.reshape(1, PAIRS_DEV)
    return pl.pallas_call(
        functools.partial(kernel, slabs),
        out_shape=jax.ShapeDtypeStruct((3, WITHIN), F32),
        in_specs=[vmem()] * 7 + [smem(), vmem()],
        out_specs=vmem(),
        scratch_shapes=[
            pltpu.VMEM((outer, 6, 4, PB), F32),
            pltpu.VMEM((outer, FAR, 16, PB), BF16),
            pltpu.VMEM((SLAB, FAR, 16, PB), BF16),
            pltpu.VMEM((SLAB, 4, 8, PB), F32),
            pltpu.VMEM((SLAB * 4, PB, 48), BF16),
            pltpu.VMEM((SLAB * 4, 16, PB), BF16),
            pltpu.VMEM((4, 8, PB), F32),
            pltpu.VMEM((4, 16, 2 * PB), BF16),
            pltpu.VMEM((4, 48, 2 * PB), BF16),
            pltpu.VMEM((8, 48, 2 * PB), BF16),
            pltpu.VMEM((outer, 4, 4, PB), F32),
            pltpu.VMEM((SLAB, 4, 4, PB), F32),
            pltpu.VMEM((outer, 4, 4, PB), F32),
            pltpu.VMEM((SLAB, 4, 4, PB), F32),
            pltpu.VMEM((4, 3, 4, PB), F32),
            pltpu.VMEM((16, 3, 4, PB), F32),
            pltpu.VMEM((SLAB, 8, PB), jnp.int32),
            pltpu.SMEM((SLAB, 8, PB), jnp.int32),
            pltpu.SemaphoreType.DMA,
            pltpu.SemaphoreType.DMA((outer,)),
            pltpu.SemaphoreType.DMA((outer,)),
            pltpu.SemaphoreType.DMA((8,)),
            pltpu.SemaphoreType.DMA((8,)),
        ],
        compiler_params=pltpu.CompilerParams(
            collective_id=0, has_side_effects=True, vmem_limit_bytes=48 * 1024 * 1024
        ),
        name="gather_pairs_return",
    )(
        panel_geometry.transpose(1, 0, 2),
        adjoint.reshape(16, PB),
        strengths.reshape(16, PB),
        row(pair_target),
        row(pair_owner),
        row(pair_source),
        row(pair_order),
        pair_count,
        corner_vertex,
    )


def solution(mesh):
    placed = (
        P("tiles", None, None),
        P("tiles", "far", None),
        P("tiles", "far", None),
        P("tiles"),
        P("tiles", None),
        P("tiles"),
        P("tiles"),
        P("tiles"),
        P("tiles", None, None),
    )
    return jax.shard_map(
        per_device, mesh=mesh, in_specs=placed, out_specs=P(None, "tiles"), check_vma=False
    )
```

```python
import functools

import jax
import jax.numpy as jnp
from jax import lax
from jax.experimental import pallas as pl
from jax.experimental.pallas import tpu as pltpu
from jax.sharding import PartitionSpec as P

SLAB = 8
FAR = 4
PB = 128
PAIRS_DEV = 32
GROUP = 8
MESH = pl.DeviceIdType.MESH
F32 = jnp.float32
BF16 = jnp.bfloat16

ROOT_HALF = 0.5773502691896258
ROOT_FIFTH = 0.7745966692414834
WITHIN = 4 * PB
def place(slabs):
    t = lax.axis_index("tiles")
    y = lax.axis_index("far")
    z = t // SLAB
    return t, z, t - z * SLAB, y, z % FAR


def send(src, dst, send_sem, recv_sem, device):
    pltpu.make_async_remote_copy(
        src_ref=src,
        dst_ref=dst,
        send_sem=send_sem,
        recv_sem=recv_sem,
        device_id=device,
        device_id_type=MESH,
    ).start()


def wait(ref, sem):
    pltpu.make_async_copy(ref, ref, sem).wait()


def split(values):
    high = values.astype(BF16).astype(F32)
    rest = values - high
    middle = rest.astype(BF16).astype(F32)
    return high, middle, (rest - middle).astype(BF16).astype(F32)


def squares(points, offset):
    total = points[0:1] * points[0:1] + points[1:2] * points[1:2] + (points[2:3] * points[2:3] + offset)
    return split(total)


def kernel(
    slabs,
    geom_ref,
    adj_ref,
    str_ref,
    tgt_ref,
    own_ref,
    src_ref,
    ord_ref,
    cnt_ref,
    corner_ref,
    out_ref,
    sgeom,
    sstr,
    tadj,
    tinfo,
    left,
    trow,
    sbase,
    srow,
    right,
    right_far,
    source_acc,
    target_acc,
    rs_source,
    rs_target,
    parts,
    landed,
    codes_v,
    codes,
    codes_sem,
    str_sems,
    geom_sems,
    send_sems,
    recv_sems,
):
    t, z, s, y, home = place(slabs)
    outer = slabs // FAR
    quarter = z // FAR
    tiles = slabs * SLAB
    mine = y == home
    other = jnp.logical_not(mine)
    barrier = pltpu.get_barrier_semaphore()
    near_first = {1: (0,), 2: (0, 1), 4: (0, 1, 3, 2)}[outer]
    shifts = (0, 1, tiles - 1, tiles // 2)

    def greet(device):
        pl.semaphore_signal(barrier, inc=1, device_id=device, device_id_type=MESH)

    for zz in range(outer):
        for dy in range(1, FAR):
            greet(((zz * FAR + y) * SLAB + s, (home + dy) % FAR))
    for dz in range(1, outer):
        greet(((((quarter + dz) % outer) * FAR + y) * SLAB + s, home))

    @pl.when(other)
    def _():
        greet(((quarter * FAR + y) * SLAB + s, home))

    for o in (3, 1, 2, 0):
        for dy in range(FAR):
            if o or dy:
                greet(((t + tiles - shifts[o]) % tiles, (y + dy) % FAR))
    for ds in range(1, SLAB):
        greet((z * SLAB + (s + ds) % SLAB, y))

    lane = lax.broadcasted_iota(jnp.int32, (1, PB), 1)
    tinfo[s] = jnp.zeros((4, 8, PB), F32)
    for comp in range(3):
        for block in range(4):
            tinfo[s, block, comp : comp + 1, :] = geom_ref[comp, block : block + 1, :]
    live = lax.broadcasted_iota(jnp.int32, (1, PAIRS_DEV), 1) < cnt_ref[0]
    orders = jnp.where(live, ord_ref[...], 0)
    for row, values in enumerate((tgt_ref[...], own_ref[...], src_ref[...], orders)):
        tinfo[s, 0, 4 + row : 5 + row, 0:PAIRS_DEV] = values.astype(F32)

    pl.semaphore_wait(barrier, slabs - mine.astype(jnp.int32) + SLAB - 1 + 15)

    def send_strengths(zt):
        da = (quarter - zt // FAR + outer) % outer
        send(str_ref, sstr.at[da, y], send_sems.at[0], str_sems.at[da], (zt * SLAB + s, home))

    def send_geometry(zt):
        da = (quarter - zt // FAR + outer) % outer
        send(geom_ref, sgeom.at[da], send_sems.at[1], geom_sems.at[da], (zt * SLAB + s, home))

    for step in range(slabs // 2, 0, -1):
        send_strengths((z + step) % slabs)
        if 2 * step != slabs:
            send_strengths((z + slabs - step) % slabs)
    for dk in near_first[::-1]:
        if dk:
            send_geometry(((quarter + dk) % outer) * FAR + y)

    @pl.when(other)
    def _():
        send_strengths(z)
        send_geometry(quarter * FAR + y)

    @pl.when(mine)
    def _():
        sstr[0, y] = str_ref[...]
        sgeom[0] = geom_ref[...]

    for dy in range(1, FAR):
        send(adj_ref, tadj.at[s, y], send_sems.at[2], recv_sems.at[2], (t, (y + dy) % FAR))
    for ds in range(1, SLAB):
        peer = (z * SLAB + (s + ds) % SLAB, y)
        send(tinfo.at[s], tinfo.at[s], send_sems.at[3], recv_sems.at[3], peer)
    tadj[s, y] = adj_ref[...]
    wait(tadj.at[s, pl.ds(0, FAR - 1)], recv_sems.at[2])
    for ds in range(1, SLAB):
        peer = (z * SLAB + (s + ds) % SLAB, y)
        send(tadj.at[s], tadj.at[s], send_sems.at[4], recv_sems.at[4], peer)

    row = lax.broadcasted_iota(jnp.int32, (PB, PB), 0)
    picks = []
    keys = []
    for block in range(4):
        vertex = corner_ref[block]
        holder = vertex // (4 * PB)
        away = holder - t
        away = jnp.where(away < 0, away + tiles, away)
        group = jnp.where(
            away == 0, 0, jnp.where(away == 1, 1, jnp.where(away == tiles - 1, 2, 3))
        )
        within = vertex - holder * (4 * PB)
        high = within // PB
        low = within - high * PB
        keys.append(group * 4 + high)
        picks += [jnp.where(row == low[j : j + 1], 1.0, 0.0).astype(BF16) for j in range(4)]
    picks = jnp.concatenate(picks, axis=1)

    wait(tinfo.at[pl.ds(0, SLAB - 1)], recv_sems.at[3])
    place_of = lax.broadcasted_iota(jnp.int32, (8, PB), 0)
    wide_lane = lax.broadcasted_iota(jnp.int32, (8, PB), 1)
    da_of = place_of // 2
    wanted = ((quarter + da_of) % outer * FAR + y) * SLAB + s
    before = jnp.where(
        lax.broadcasted_iota(jnp.int32, (PB, PB), 0) < lax.broadcasted_iota(jnp.int32, (PB, PB), 1), 1.0, 0.0
    ).astype(BF16)
    for k in range(SLAB):
        rows = tinfo[k, 0].astype(jnp.int32)
        target, owner, source, order = (rows[r : r + 1] for r in range(4, 8))
        match = (owner == wanted) & (order > 0) & (wide_lane < PAIRS_DEV) & (da_of < outer)
        count = jnp.dot(
            jnp.where(match, 1.0, 0.0).astype(BF16), before, preferred_element_type=F32
        ).astype(jnp.int32)
        code = (target * 4 + source) * 4 + order
        chosen = jnp.where(match & (count == place_of - 2 * da_of), code, 0).astype(F32)
        total = jnp.sum(chosen, axis=1, keepdims=True).astype(jnp.int32)
        codes_v[k] = jnp.broadcast_to(total, (8, PB))
    copy = pltpu.make_async_copy(codes_v, codes, codes_sem)
    copy.start()

    wait(tadj.at[pl.ds(0, SLAB - 1)], recv_sems.at[4])
    zero4 = jnp.zeros((4, PB), F32)
    one = jnp.ones((1, PB), F32)
    zero1 = jnp.zeros((1, PB), F32)

    def prepare_list(k, carry):
        conditions = [tadj[k, yy].astype(F32) for yy in range(FAR)]
        for block in range(4):
            centre = tinfo[k, block][0:4]
            high, middle, low = split(centre)
            sq = squares(centre, 0.0)
            stack = jnp.concatenate(
                [c[4 * block : 4 * block + 4] for c in conditions]
                + [high, high, high, middle, middle, low]
                + [*sq, one, one, one, zero1, zero1],
                axis=0,
            )
            left[k * 4 + block] = stack.T.astype(BF16)
            trow[k * 4 + block] = jnp.concatenate(
                [one, zero1, zero1, zero1, high, middle, low], axis=0
            ).astype(BF16)
        target_acc[k] = jnp.zeros((4, 4, PB), F32)
        return carry

    lax.fori_loop(0, SLAB, prepare_list, 0)
    copy.wait()

    for da in near_first:
        if da:
            wait(sstr.at[da], str_sems.at[da])
            wait(sgeom.at[da], geom_sems.at[da])
        else:

            @pl.when(mine)
            def _():
                wait(sstr.at[0, pl.ds(0, FAR - 1)], str_sems.at[0])

            @pl.when(other)
            def _():
                wait(sstr.at[0], str_sems.at[0])
                wait(sgeom.at[0], geom_sems.at[0])

        conditions = [sstr[da, yy].astype(F32) for yy in range(FAR)]
        for block in range(4):
            base = jnp.concatenate([sgeom[da, c, block : block + 1, :] for c in range(3)] + [zero1], axis=0)
            half = 0.25 * jnp.concatenate(
                [sgeom[da, 3 + c, block : block + 1, :] for c in range(3)] + [zero1], axis=0
            )
            sbase[block] = jnp.concatenate([base, half], axis=0)
            first, second = split(base), split(half)
            srow[block] = jnp.concatenate(
                [
                    jnp.concatenate([one, zero1, zero1, zero1, *first], axis=0),
                    jnp.concatenate([zero4, *second], axis=0),
                ],
                axis=1,
            ).astype(BF16)

            def distance(points):
                high, middle, low = (-2.0 * part for part in split(points))
                sq = squares(points, 0.0625)
                return jnp.concatenate(
                    [zero4] * 4
                    + [high, middle, low, high, middle, high]
                    + [one, one, one, *sq, zero1, zero1],
                    axis=0,
                )

            coupled = jnp.concatenate(
                [c[4 * block : 4 * block + 4] for c in conditions] + [zero4] * 8, axis=0
            )
            right[block] = jnp.concatenate([coupled, distance(base)], axis=1).astype(BF16)
            for rule, node in enumerate((ROOT_HALF, ROOT_FIFTH)):
                right_far[block * 2 + rule] = jnp.concatenate(
                    [distance(base + node * half), distance(base - node * half)], axis=1
                ).astype(BF16)
        source_acc[da] = jnp.zeros((4, 4, PB), F32)

        def some_lists(group, carry, da=da):
            slots = []
            for step in range(GROUP):
                k = group * GROUP + step
                for occurrence in range(2):
                    code = codes[k, 2 * da + occurrence, 0]
                    slots.append((k, code & 3, (code >> 2) & 3, (code >> 4) & 3))
            products = []
            for k, order, source, target in slots:
                columns = left[k * 4 + target]
                products.append(
                    (
                        jnp.dot(columns, right[source], preferred_element_type=F32),
                        jnp.dot(
                            columns,
                            right_far[source * 2 + ((order + 1) >> 2)],
                            preferred_element_type=F32,
                        ),
                    )
                )
            factors = []
            for (k, order, source, target), (inner, sides) in zip(slots, products):
                centre_weight = jnp.where(order == 1, 1.0, jnp.where(order == 3, 4.0 / 9.0, 0.0))
                side_weight = jnp.where(order == 2, 0.5, jnp.where(order == 3, 5.0 / 18.0, 0.0))
                shift_weight = jnp.where(
                    order == 2, 0.5 * ROOT_HALF, jnp.where(order == 3, 5.0 / 18.0 * ROOT_FIFTH, 0.0)
                )
                roots = lax.rsqrt(inner[:, PB:])
                pulls = lax.rsqrt(sides)
                roots = roots * roots * roots
                pulls = pulls * pulls * pulls
                coupling = inner[:, :PB]
                plus, minus = pulls[:, :PB], pulls[:, PB:]
                both = coupling * (centre_weight * roots + side_weight * (plus + minus))
                skew = (shift_weight * coupling) * (plus - minus)
                high = jnp.concatenate([both.astype(BF16), skew.astype(BF16)], axis=1)
                low = jnp.concatenate(
                    [
                        (both - high[:, :PB].astype(F32)).astype(BF16),
                        (skew - high[:, PB:].astype(F32)).astype(BF16),
                    ],
                    axis=1,
                )
                factors.append((high, low))
            sums = []
            across = (((1,), (1,)), ((), ()))
            for (k, order, source, target), (high, low) in zip(slots, factors):
                rows, lines = trow[k * 4 + target], srow[source]
                sums.append(
                    (
                        jnp.dot(rows, high, preferred_element_type=F32)
                        + jnp.dot(rows, low, preferred_element_type=F32),
                        lax.dot_general(lines, high, across, preferred_element_type=F32)
                        + lax.dot_general(lines, low, across, preferred_element_type=F32),
                    )
                )
            gathered = [source_acc[da, block] for block in range(4)]
            returned = [None] * 4
            for n, ((k, order, source, target), (by_source, by_target)) in enumerate(zip(slots, sums)):
                points = sbase[source]
                pulled = (
                    by_source[4:8, :PB]
                    + by_source[8:12, :PB]
                    + by_source[12:16, :PB]
                    - points[0:4] * by_source[0:1, :PB]
                    - points[4:8] * by_source[0:1, PB:]
                )
                pushed = (
                    by_target[4:8]
                    + by_target[8:12]
                    + by_target[12:16]
                    - tinfo[k, target][0:4] * by_target[0:1]
                )
                for block in range(4):
                    gathered[block] = gathered[block] + jnp.where(source == block, 1.0, 0.0) * pulled
                    term = jnp.where(target == block, 1.0, 0.0) * pushed
                    returned[block] = term if n % 2 == 0 else returned[block] + term
                if n % 2:
                    for block in range(4):
                        target_acc[k, block] += returned[block]
            for block in range(4):
                source_acc[da, block] = gathered[block]
            return carry

        lax.fori_loop(0, SLAB // GROUP, some_lists, 0)

        def send_source(da=da):
            send(
                source_acc.at[da],
                rs_source.at[quarter],
                send_sems.at[5],
                recv_sems.at[5],
                ((((quarter + da) % outer) * FAR + y) * SLAB + s, home),
            )

        if da:
            send_source()
        else:
            pl.when(other)(send_source)

            @pl.when(mine)
            def _():
                rs_source[quarter] = source_acc[0]

    for ds in range(1, SLAB):
        st = (s + ds) % SLAB
        send(target_acc.at[st], rs_target.at[s], send_sems.at[6], recv_sems.at[6], (z * SLAB + st, y))
    rs_target[s] = target_acc[s]
    wait(rs_target.at[pl.ds(0, SLAB - 1)], recv_sems.at[6])

    @pl.when(mine)
    def _():
        if outer > 1:
            wait(rs_source.at[pl.ds(0, outer - 1)], recv_sems.at[5])

    @pl.when(other)
    def _():
        wait(rs_source.at[pl.ds(0, outer)], recv_sems.at[5])

    grad = jnp.sum(rs_target[...], axis=0) + jnp.sum(rs_source[...], axis=0)
    grad = grad * (0.25 * 0.0078125)
    rowkey = lax.broadcasted_iota(jnp.int32, (16, PB), 0)
    upper = [[], [], []]
    lower = [[], [], []]
    for block in range(4):
        for c in range(3):
            wide = jnp.broadcast_to(grad[block, c : c + 1], (16, PB))
            first = wide.astype(BF16)
            second = (wide - first.astype(F32)).astype(BF16)
            for j in range(4):
                here = rowkey == keys[block][j : j + 1]
                upper[c].append(jnp.where(here, first, jnp.zeros_like(first)))
                lower[c].append(jnp.where(here, second, jnp.zeros_like(second)))
    spread = jnp.concatenate([jnp.concatenate(part, axis=1) for part in upper + lower], axis=0)
    sums = lax.dot_general(spread, picks, (((1,), (1,)), ((), ())), preferred_element_type=F32)
    sums = sums[0:48] + sums[48:96]
    for o in range(4):
        for c in range(3):
            parts[o, c] = sums[16 * c + 4 * o : 16 * c + 4 * o + 4]
    for o in (3, 1, 2, 0):
        for dy in range(FAR):
            if o or dy:
                send(
                    parts.at[o],
                    landed.at[o * FAR + dy],
                    send_sems.at[7],
                    recv_sems.at[7],
                    ((t + shifts[o]) % tiles, (y + dy) % FAR),
                )
    landed[0] = parts[0]
    wait(landed.at[pl.ds(1, 15)], recv_sems.at[7])
    result = jnp.sum(landed[...], axis=0)
    for k in range(4):
        for c in range(3):
            out_ref[c : c + 1, k * PB : (k + 1) * PB] = result[c, k : k + 1]

    wait(tadj.at[s, pl.ds(0, FAR - 1)], send_sems.at[2])
    wait(tinfo.at[pl.ds(0, SLAB - 1)], send_sems.at[3])
    wait(tadj.at[pl.ds(0, SLAB - 1)], send_sems.at[4])
    wait(rs_target.at[pl.ds(0, SLAB - 1)], send_sems.at[6])
    wait(landed.at[pl.ds(1, 15)], send_sems.at[7])

    @pl.when(mine)
    def _():
        if outer > 1:
            wait(sstr.at[pl.ds(0, outer - 1)], send_sems.at[0])
            wait(sgeom.at[pl.ds(0, outer - 1)], send_sems.at[1])
            wait(rs_source.at[pl.ds(0, outer - 1)], send_sems.at[5])
        wait(sstr.at[0, pl.ds(0, FAR - 1)], send_sems.at[0])

    @pl.when(other)
    def _():
        wait(sstr, send_sems.at[0])
        wait(sgeom, send_sems.at[1])
        wait(rs_source, send_sems.at[5])


def vmem():
    return pl.BlockSpec(memory_space=pltpu.VMEM)


def smem():
    return pl.BlockSpec(memory_space=pltpu.SMEM)


def per_device(
    panel_geometry,
    adjoint,
    strengths,
    pair_target,
    pair_owner,
    pair_source,
    pair_order,
    pair_count,
    corner_vertex,
):
    slabs = lax.axis_size("tiles") // SLAB
    outer = slabs // FAR
    row = lambda values: values.reshape(1, PAIRS_DEV)
    return pl.pallas_call(
        functools.partial(kernel, slabs),
        out_shape=jax.ShapeDtypeStruct((3, WITHIN), F32),
        in_specs=[vmem()] * 7 + [smem(), vmem()],
        out_specs=vmem(),
        scratch_shapes=[
            pltpu.VMEM((outer, 6, 4, PB), F32),
            pltpu.VMEM((outer, FAR, 16, PB), BF16),
            pltpu.VMEM((SLAB, FAR, 16, PB), BF16),
            pltpu.VMEM((SLAB, 4, 8, PB), F32),
            pltpu.VMEM((SLAB * 4, PB, 48), BF16),
            pltpu.VMEM((SLAB * 4, 16, PB), BF16),
            pltpu.VMEM((4, 8, PB), F32),
            pltpu.VMEM((4, 16, 2 * PB), BF16),
            pltpu.VMEM((4, 48, 2 * PB), BF16),
            pltpu.VMEM((8, 48, 2 * PB), BF16),
            pltpu.VMEM((outer, 4, 4, PB), F32),
            pltpu.VMEM((SLAB, 4, 4, PB), F32),
            pltpu.VMEM((outer, 4, 4, PB), F32),
            pltpu.VMEM((SLAB, 4, 4, PB), F32),
            pltpu.VMEM((4, 3, 4, PB), F32),
            pltpu.VMEM((16, 3, 4, PB), F32),
            pltpu.VMEM((SLAB, 8, PB), jnp.int32),
            pltpu.SMEM((SLAB, 8, PB), jnp.int32),
            pltpu.SemaphoreType.DMA,
            pltpu.SemaphoreType.DMA((outer,)),
            pltpu.SemaphoreType.DMA((outer,)),
            pltpu.SemaphoreType.DMA((8,)),
            pltpu.SemaphoreType.DMA((8,)),
        ],
        compiler_params=pltpu.CompilerParams(
            collective_id=0, has_side_effects=True
        ),
        name="gather_pairs_return",
    )(
        panel_geometry.transpose(1, 0, 2),
        adjoint.reshape(16, PB),
        strengths.reshape(16, PB),
        row(pair_target),
        row(pair_owner),
        row(pair_source),
        row(pair_order),
        pair_count,
        corner_vertex,
    )


def solution(mesh):
    placed = (
        P("tiles", None, None),
        P("tiles", "far", None),
        P("tiles", "far", None),
        P("tiles"),
        P("tiles", None),
        P("tiles"),
        P("tiles"),
        P("tiles"),
        P("tiles", None, None),
    )
    return jax.shard_map(
        per_device, mesh=mesh, in_specs=placed, out_specs=P(None, "tiles"), check_vma=False
    )
```

```python
import functools

import jax
import jax.numpy as jnp
from jax import lax
from jax.experimental import pallas as pl
from jax.experimental.pallas import tpu as pltpu
from jax.sharding import PartitionSpec as P

SLAB = 8
FAR = 4
PB = 128
PAIRS_DEV = 32
GROUP = 8
MESH = pl.DeviceIdType.MESH
F32 = jnp.float32
BF16 = jnp.bfloat16

ROOT_HALF = 0.5773502691896258
ROOT_FIFTH = 0.7745966692414834
WITHIN = 4 * PB
def place(slabs):
    t = lax.axis_index("tiles")
    y = lax.axis_index("far")
    z = t // SLAB
    return t, z, t - z * SLAB, y, z % FAR


def send(src, dst, send_sem, recv_sem, device):
    pltpu.make_async_remote_copy(
        src_ref=src,
        dst_ref=dst,
        send_sem=send_sem,
        recv_sem=recv_sem,
        device_id=device,
        device_id_type=MESH,
    ).start()


def wait(ref, sem):
    pltpu.make_async_copy(ref, ref, sem).wait()


def split(values):
    high = values.astype(BF16).astype(F32)
    rest = values - high
    middle = rest.astype(BF16).astype(F32)
    return high, middle, (rest - middle).astype(BF16).astype(F32)


def squares(points, offset):
    total = points[0:1] * points[0:1] + points[1:2] * points[1:2] + (points[2:3] * points[2:3] + offset)
    return split(total)


def kernel(
    slabs,
    geom_in,
    adj_in,
    str_in,
    tgt_in,
    own_in,
    src_in,
    ord_in,
    cnt_ref,
    corner_in,
    out_ref,
    geom_ref,
    adj_ref,
    str_ref,
    tgt_ref,
    own_ref,
    src_ref,
    ord_ref,
    corner_ref,
    load_sems,
    sgeom,
    sstr,
    tadj,
    tinfo,
    left,
    trow,
    sbase,
    srow,
    right,
    right_far,
    source_acc,
    target_acc,
    rs_source,
    rs_target,
    parts,
    landed,
    codes_v,
    codes,
    codes_sem,
    str_sems,
    geom_sems,
    send_sems,
    recv_sems,
):
    t, z, s, y, home = place(slabs)
    outer = slabs // FAR
    quarter = z // FAR
    tiles = slabs * SLAB
    mine = y == home
    other = jnp.logical_not(mine)
    barrier = pltpu.get_barrier_semaphore()
    near_first = {1: (0,), 2: (0, 1), 4: (0, 1, 3, 2)}[outer]
    near_last = {1: (0,), 2: (1, 0), 4: (1, 3, 2, 0)}[outer]
    shifts = (0, 1, tiles - 1, tiles // 2)

    loads = [
        pltpu.make_async_copy(src, dst, load_sems.at[n])
        for n, (src, dst) in enumerate(
            (
                (geom_in, geom_ref),
                (tgt_in, tgt_ref),
                (own_in, own_ref),
                (src_in, src_ref),
                (ord_in, ord_ref),
                (str_in, str_ref),
                (adj_in, adj_ref),
                (corner_in, corner_ref),
            )
        )
    ]
    for load in loads:
        load.start()

    def greet(device):
        pl.semaphore_signal(barrier, inc=1, device_id=device, device_id_type=MESH)

    for zz in range(outer):
        for dy in range(1, FAR):
            greet(((zz * FAR + y) * SLAB + s, (home + dy) % FAR))
    for dz in range(1, outer):
        greet(((((quarter + dz) % outer) * FAR + y) * SLAB + s, home))

    @pl.when(other)
    def _():
        greet(((quarter * FAR + y) * SLAB + s, home))

    for o in (3, 1, 2, 0):
        for dy in range(FAR):
            if o or dy:
                greet(((t + tiles - shifts[o]) % tiles, (y + dy) % FAR))
    for ds in range(1, SLAB):
        greet((z * SLAB + (s + ds) % SLAB, y))

    for load in loads:
        load.wait()

    lane = lax.broadcasted_iota(jnp.int32, (1, PB), 1)
    tinfo[s] = jnp.zeros((4, 8, PB), F32)
    for comp in range(3):
        for block in range(4):
            tinfo[s, block, comp : comp + 1, :] = geom_ref[comp, block : block + 1, :]
    live = lax.broadcasted_iota(jnp.int32, (1, PAIRS_DEV), 1) < cnt_ref[0]
    orders = jnp.where(live, ord_ref[...], 0)
    for row, values in enumerate((tgt_ref[...], own_ref[...], src_ref[...], orders)):
        tinfo[s, 0, 4 + row : 5 + row, 0:PAIRS_DEV] = values.astype(F32)

    pl.semaphore_wait(barrier, slabs - mine.astype(jnp.int32) + SLAB - 1 + 15)

    for dy in range(1, FAR):
        send(adj_ref, tadj.at[s, y], send_sems.at[2], recv_sems.at[2], (t, (y + dy) % FAR))
    tadj[s, y] = adj_ref[...]

    def send_strengths(zt):
        da = (quarter - zt // FAR + outer) % outer
        send(str_ref, sstr.at[da, y], send_sems.at[0], str_sems.at[da], (zt * SLAB + s, home))

    def send_geometry(zt):
        da = (quarter - zt // FAR + outer) % outer
        send(geom_ref, sgeom.at[da], send_sems.at[1], geom_sems.at[da], (zt * SLAB + s, home))

    for step in range(slabs // 2, 0, -1):
        send_strengths((z + step) % slabs)
        if 2 * step != slabs:
            send_strengths((z + slabs - step) % slabs)
    for dk in near_first[::-1]:
        if dk:
            send_geometry(((quarter + dk) % outer) * FAR + y)

    @pl.when(other)
    def _():
        send_strengths(z)
        send_geometry(quarter * FAR + y)

    @pl.when(mine)
    def _():
        sstr[0, y] = str_ref[...]
        sgeom[0] = geom_ref[...]

    for ds in range(1, SLAB):
        peer = (z * SLAB + (s + ds) % SLAB, y)
        send(tinfo.at[s], tinfo.at[s], send_sems.at[3], recv_sems.at[3], peer)
    wait(tadj.at[s, pl.ds(0, FAR - 1)], recv_sems.at[2])
    for ds in range(1, SLAB):
        peer = (z * SLAB + (s + ds) % SLAB, y)
        send(tadj.at[s], tadj.at[s], send_sems.at[4], recv_sems.at[4], peer)

    row = lax.broadcasted_iota(jnp.int32, (PB, PB), 0)
    picks = []
    keys = []
    for block in range(4):
        vertex = corner_ref[block]
        holder = vertex // (4 * PB)
        away = holder - t
        away = jnp.where(away < 0, away + tiles, away)
        group = jnp.where(
            away == 0, 0, jnp.where(away == 1, 1, jnp.where(away == tiles - 1, 2, 3))
        )
        within = vertex - holder * (4 * PB)
        high = within // PB
        low = within - high * PB
        keys.append(group * 4 + high)
        picks += [jnp.where(row == low[j : j + 1], 1.0, 0.0).astype(BF16) for j in range(4)]
    picks = jnp.concatenate(picks, axis=1)

    wait(tinfo.at[pl.ds(0, SLAB - 1)], recv_sems.at[3])
    place_of = lax.broadcasted_iota(jnp.int32, (8, PB), 0)
    wide_lane = lax.broadcasted_iota(jnp.int32, (8, PB), 1)
    da_of = place_of // 2
    wanted = ((quarter + da_of) % outer * FAR + y) * SLAB + s
    before = jnp.where(
        lax.broadcasted_iota(jnp.int32, (PB, PB), 0) < lax.broadcasted_iota(jnp.int32, (PB, PB), 1), 1.0, 0.0
    ).astype(BF16)
    for k in range(SLAB):
        rows = tinfo[k, 0].astype(jnp.int32)
        target, owner, source, order = (rows[r : r + 1] for r in range(4, 8))
        match = (owner == wanted) & (order > 0) & (wide_lane < PAIRS_DEV) & (da_of < outer)
        count = jnp.dot(
            jnp.where(match, 1.0, 0.0).astype(BF16), before, preferred_element_type=F32
        ).astype(jnp.int32)
        code = (target * 4 + source) * 4 + order
        chosen = jnp.where(match & (count == place_of - 2 * da_of), code, 0).astype(F32)
        total = jnp.sum(chosen, axis=1, keepdims=True).astype(jnp.int32)
        codes_v[k] = jnp.broadcast_to(total, (8, PB))
    copy = pltpu.make_async_copy(codes_v, codes, codes_sem)
    copy.start()

    wait(tadj.at[pl.ds(0, SLAB - 1)], recv_sems.at[4])
    zero4 = jnp.zeros((4, PB), F32)
    one = jnp.ones((1, PB), F32)
    zero1 = jnp.zeros((1, PB), F32)

    def prepare_list(k, carry):
        conditions = [tadj[k, yy].astype(F32) for yy in range(FAR)]
        for block in range(4):
            centre = tinfo[k, block][0:4]
            high, middle, low = split(centre)
            sq = squares(centre, 0.0)
            stack = jnp.concatenate(
                [c[4 * block : 4 * block + 4] for c in conditions]
                + [high, high, high, middle, middle, low]
                + [*sq, one, one, one, zero1, zero1],
                axis=0,
            )
            left[k * 4 + block] = stack.T.astype(BF16)
            trow[k * 4 + block] = jnp.concatenate(
                [one, zero1, zero1, zero1, high, middle, low], axis=0
            ).astype(BF16)
        target_acc[k] = jnp.zeros((4, 4, PB), F32)
        return carry

    lax.fori_loop(0, SLAB, prepare_list, 0)
    copy.wait()

    for da in near_last:
        if da:
            wait(sstr.at[da], str_sems.at[da])
            wait(sgeom.at[da], geom_sems.at[da])
        else:

            @pl.when(mine)
            def _():
                wait(sstr.at[0, pl.ds(0, FAR - 1)], str_sems.at[0])

            @pl.when(other)
            def _():
                wait(sstr.at[0], str_sems.at[0])
                wait(sgeom.at[0], geom_sems.at[0])

        conditions = [sstr[da, yy].astype(F32) for yy in range(FAR)]
        for block in range(4):
            base = jnp.concatenate([sgeom[da, c, block : block + 1, :] for c in range(3)] + [zero1], axis=0)
            half = 0.25 * jnp.concatenate(
                [sgeom[da, 3 + c, block : block + 1, :] for c in range(3)] + [zero1], axis=0
            )
            sbase[block] = jnp.concatenate([base, half], axis=0)
            first, second = split(base), split(half)
            srow[block] = jnp.concatenate(
                [
                    jnp.concatenate([one, zero1, zero1, zero1, *first], axis=0),
                    jnp.concatenate([zero4, *second], axis=0),
                ],
                axis=1,
            ).astype(BF16)

            def distance(points):
                high, middle, low = (-2.0 * part for part in split(points))
                sq = squares(points, 0.0625)
                return jnp.concatenate(
                    [zero4] * 4
                    + [high, middle, low, high, middle, high]
                    + [one, one, one, *sq, zero1, zero1],
                    axis=0,
                )

            coupled = jnp.concatenate(
                [c[4 * block : 4 * block + 4] for c in conditions] + [zero4] * 8, axis=0
            )
            right[block] = jnp.concatenate([coupled, distance(base)], axis=1).astype(BF16)
            for rule, node in enumerate((ROOT_HALF, ROOT_FIFTH)):
                right_far[block * 2 + rule] = jnp.concatenate(
                    [distance(base + node * half), distance(base - node * half)], axis=1
                ).astype(BF16)
        source_acc[da] = jnp.zeros((4, 4, PB), F32)

        def some_lists(group, carry, da=da):
            slots = []
            for step in range(GROUP):
                k = group * GROUP + step
                for occurrence in range(2):
                    code = codes[k, 2 * da + occurrence, 0]
                    slots.append((k, code & 3, (code >> 2) & 3, (code >> 4) & 3))
            products = []
            for k, order, source, target in slots:
                columns = left[k * 4 + target]
                products.append(
                    (
                        jnp.dot(columns, right[source], preferred_element_type=F32),
                        jnp.dot(
                            columns,
                            right_far[source * 2 + ((order + 1) >> 2)],
                            preferred_element_type=F32,
                        ),
                    )
                )
            factors = []
            for (k, order, source, target), (inner, sides) in zip(slots, products):
                centre_weight = jnp.where(order == 1, 1.0, jnp.where(order == 3, 4.0 / 9.0, 0.0))
                side_weight = jnp.where(order == 2, 0.5, jnp.where(order == 3, 5.0 / 18.0, 0.0))
                shift_weight = jnp.where(
                    order == 2, 0.5 * ROOT_HALF, jnp.where(order == 3, 5.0 / 18.0 * ROOT_FIFTH, 0.0)
                )
                roots = lax.rsqrt(inner[:, PB:])
                pulls = lax.rsqrt(sides)
                roots = roots * roots * roots
                pulls = pulls * pulls * pulls
                coupling = inner[:, :PB]
                plus, minus = pulls[:, :PB], pulls[:, PB:]
                both = coupling * (centre_weight * roots + side_weight * (plus + minus))
                skew = (shift_weight * coupling) * (plus - minus)
                high = jnp.concatenate([both.astype(BF16), skew.astype(BF16)], axis=1)
                low = jnp.concatenate(
                    [
                        (both - high[:, :PB].astype(F32)).astype(BF16),
                        (skew - high[:, PB:].astype(F32)).astype(BF16),
                    ],
                    axis=1,
                )
                factors.append((high, low))
            sums = []
            across = (((1,), (1,)), ((), ()))
            for (k, order, source, target), (high, low) in zip(slots, factors):
                rows, lines = trow[k * 4 + target], srow[source]
                sums.append(
                    (
                        jnp.dot(rows, high, preferred_element_type=F32)
                        + jnp.dot(rows, low, preferred_element_type=F32),
                        lax.dot_general(lines, high, across, preferred_element_type=F32)
                        + lax.dot_general(lines, low, across, preferred_element_type=F32),
                    )
                )
            gathered = [source_acc[da, block] for block in range(4)]
            returned = [None] * 4
            for n, ((k, order, source, target), (by_source, by_target)) in enumerate(zip(slots, sums)):
                points = sbase[source]
                pulled = (
                    by_source[4:8, :PB]
                    + by_source[8:12, :PB]
                    + by_source[12:16, :PB]
                    - points[0:4] * by_source[0:1, :PB]
                    - points[4:8] * by_source[0:1, PB:]
                )
                pushed = (
                    by_target[4:8]
                    + by_target[8:12]
                    + by_target[12:16]
                    - tinfo[k, target][0:4] * by_target[0:1]
                )
                for block in range(4):
                    gathered[block] = gathered[block] + jnp.where(source == block, 1.0, 0.0) * pulled
                    term = jnp.where(target == block, 1.0, 0.0) * pushed
                    returned[block] = term if n % 2 == 0 else returned[block] + term
                if n % 2:
                    for block in range(4):
                        target_acc[k, block] += returned[block]
            for block in range(4):
                source_acc[da, block] = gathered[block]
            return carry

        lax.fori_loop(0, SLAB // GROUP, some_lists, 0)

        def send_source(da=da):
            send(
                source_acc.at[da],
                rs_source.at[quarter],
                send_sems.at[5],
                recv_sems.at[5],
                ((((quarter + da) % outer) * FAR + y) * SLAB + s, home),
            )

        if da:
            send_source()
        else:
            pl.when(other)(send_source)

            @pl.when(mine)
            def _():
                rs_source[quarter] = source_acc[0]

    for ds in range(1, SLAB):
        st = (s + ds) % SLAB
        send(target_acc.at[st], rs_target.at[s], send_sems.at[6], recv_sems.at[6], (z * SLAB + st, y))
    rs_target[s] = target_acc[s]
    wait(rs_target.at[pl.ds(0, SLAB - 1)], recv_sems.at[6])

    @pl.when(mine)
    def _():
        if outer > 1:
            wait(rs_source.at[pl.ds(0, outer - 1)], recv_sems.at[5])

    @pl.when(other)
    def _():
        wait(rs_source.at[pl.ds(0, outer)], recv_sems.at[5])

    grad = jnp.sum(rs_target[...], axis=0) + jnp.sum(rs_source[...], axis=0)
    grad = grad * (0.25 * 0.0078125)
    rowkey = lax.broadcasted_iota(jnp.int32, (16, PB), 0)
    upper = [[], [], []]
    lower = [[], [], []]
    for block in range(4):
        for c in range(3):
            wide = jnp.broadcast_to(grad[block, c : c + 1], (16, PB))
            first = wide.astype(BF16)
            second = (wide - first.astype(F32)).astype(BF16)
            for j in range(4):
                here = rowkey == keys[block][j : j + 1]
                upper[c].append(jnp.where(here, first, jnp.zeros_like(first)))
                lower[c].append(jnp.where(here, second, jnp.zeros_like(second)))
    spread = jnp.concatenate([jnp.concatenate(part, axis=1) for part in upper + lower], axis=0)
    sums = lax.dot_general(spread, picks, (((1,), (1,)), ((), ())), preferred_element_type=F32)
    sums = sums[0:48] + sums[48:96]
    for o in range(4):
        for c in range(3):
            parts[o, c] = sums[16 * c + 4 * o : 16 * c + 4 * o + 4]
    for o in (3, 1, 2, 0):
        for dy in range(FAR):
            if o or dy:
                send(
                    parts.at[o],
                    landed.at[o * FAR + dy],
                    send_sems.at[7],
                    recv_sems.at[7],
                    ((t + shifts[o]) % tiles, (y + dy) % FAR),
                )
    landed[0] = parts[0]
    wait(landed.at[pl.ds(1, 15)], recv_sems.at[7])
    result = jnp.sum(landed[...], axis=0)
    for k in range(4):
        for c in range(3):
            out_ref[c : c + 1, k * PB : (k + 1) * PB] = result[c, k : k + 1]

    wait(tadj.at[s, pl.ds(0, FAR - 1)], send_sems.at[2])
    wait(tinfo.at[pl.ds(0, SLAB - 1)], send_sems.at[3])
    wait(tadj.at[pl.ds(0, SLAB - 1)], send_sems.at[4])
    wait(rs_target.at[pl.ds(0, SLAB - 1)], send_sems.at[6])
    wait(landed.at[pl.ds(1, 15)], send_sems.at[7])

    @pl.when(mine)
    def _():
        if outer > 1:
            wait(sstr.at[pl.ds(0, outer - 1)], send_sems.at[0])
            wait(sgeom.at[pl.ds(0, outer - 1)], send_sems.at[1])
            wait(rs_source.at[pl.ds(0, outer - 1)], send_sems.at[5])
        wait(sstr.at[0, pl.ds(0, FAR - 1)], send_sems.at[0])

    @pl.when(other)
    def _():
        wait(sstr, send_sems.at[0])
        wait(sgeom, send_sems.at[1])
        wait(rs_source, send_sems.at[5])


def resident(dims, dtype):
    return pltpu.VMEM(dims, dtype)


def vmem():
    return pl.BlockSpec(memory_space=pltpu.VMEM)


def anywhere():
    return pl.BlockSpec(memory_space=pl.ANY)


def smem():
    return pl.BlockSpec(memory_space=pltpu.SMEM)


def per_device(
    panel_geometry,
    adjoint,
    strengths,
    pair_target,
    pair_owner,
    pair_source,
    pair_order,
    pair_count,
    corner_vertex,
):
    slabs = lax.axis_size("tiles") // SLAB
    outer = slabs // FAR
    row = lambda values: values.reshape(1, PAIRS_DEV)
    return pl.pallas_call(
        functools.partial(kernel, slabs),
        out_shape=resident((3, WITHIN), F32),
        in_specs=[anywhere()] * 7 + [smem(), anywhere()],
        out_specs=vmem(),
        scratch_shapes=[
            pltpu.VMEM((6, 4, PB), F32),
            pltpu.VMEM((16, PB), BF16),
            pltpu.VMEM((16, PB), BF16),
            pltpu.VMEM((1, PAIRS_DEV), jnp.int32),
            pltpu.VMEM((1, PAIRS_DEV), jnp.int32),
            pltpu.VMEM((1, PAIRS_DEV), jnp.int32),
            pltpu.VMEM((1, PAIRS_DEV), jnp.int32),
            pltpu.VMEM((4, 4, PB), jnp.int32),
            pltpu.SemaphoreType.DMA((8,)),
            pltpu.VMEM((outer, 6, 4, PB), F32),
            pltpu.VMEM((outer, FAR, 16, PB), BF16),
            pltpu.VMEM((SLAB, FAR, 16, PB), BF16),
            pltpu.VMEM((SLAB, 4, 8, PB), F32),
            pltpu.VMEM((SLAB * 4, PB, 48), BF16),
            pltpu.VMEM((SLAB * 4, 16, PB), BF16),
            pltpu.VMEM((4, 8, PB), F32),
            pltpu.VMEM((4, 16, 2 * PB), BF16),
            pltpu.VMEM((4, 48, 2 * PB), BF16),
            pltpu.VMEM((8, 48, 2 * PB), BF16),
            pltpu.VMEM((outer, 4, 4, PB), F32),
            pltpu.VMEM((SLAB, 4, 4, PB), F32),
            pltpu.VMEM((outer, 4, 4, PB), F32),
            pltpu.VMEM((SLAB, 4, 4, PB), F32),
            pltpu.VMEM((4, 3, 4, PB), F32),
            pltpu.VMEM((16, 3, 4, PB), F32),
            pltpu.VMEM((SLAB, 8, PB), jnp.int32),
            pltpu.SMEM((SLAB, 8, PB), jnp.int32),
            pltpu.SemaphoreType.DMA,
            pltpu.SemaphoreType.DMA((outer,)),
            pltpu.SemaphoreType.DMA((outer,)),
            pltpu.SemaphoreType.DMA((8,)),
            pltpu.SemaphoreType.DMA((8,)),
        ],
        compiler_params=pltpu.CompilerParams(
            collective_id=0, has_side_effects=True
        ),
        name="gather_pairs_return",
    )(
        panel_geometry.transpose(1, 0, 2),
        adjoint.reshape(16, PB),
        strengths.reshape(16, PB),
        row(pair_target),
        row(pair_owner),
        row(pair_source),
        row(pair_order),
        pair_count,
        corner_vertex,
    )


def solution(mesh):
    placed = (
        P("tiles", None, None),
        P("tiles", "far", None),
        P("tiles", "far", None),
        P("tiles"),
        P("tiles", None),
        P("tiles"),
        P("tiles"),
        P("tiles"),
        P("tiles", None, None),
    )
    return jax.shard_map(
        per_device, mesh=mesh, in_specs=placed, out_specs=P(None, "tiles"), check_vma=False
    )
```

```python
import functools

import jax
import jax.numpy as jnp
from jax import lax
from jax.experimental import pallas as pl
from jax.experimental.pallas import tpu as pltpu
from jax.sharding import PartitionSpec as P

SLAB = 8
FAR = 4
PB = 128
PAIRS_DEV = 32
GROUP = 8
MESH = pl.DeviceIdType.MESH
F32 = jnp.float32
BF16 = jnp.bfloat16

ROOT_HALF = 0.5773502691896258
ROOT_FIFTH = 0.7745966692414834
WITHIN = 4 * PB
def place(slabs):
    t = lax.axis_index("tiles")
    y = lax.axis_index("far")
    z = t // SLAB
    return t, z, t - z * SLAB, y, z % FAR


def send(src, dst, send_sem, recv_sem, device):
    pltpu.make_async_remote_copy(
        src_ref=src,
        dst_ref=dst,
        send_sem=send_sem,
        recv_sem=recv_sem,
        device_id=device,
        device_id_type=MESH,
    ).start()


def wait(ref, sem):
    pltpu.make_async_copy(ref, ref, sem).wait()


def split(values):
    high = values.astype(BF16).astype(F32)
    rest = values - high
    middle = rest.astype(BF16).astype(F32)
    return high, middle, (rest - middle).astype(BF16).astype(F32)


def squares(points, offset):
    total = points[0:1] * points[0:1] + points[1:2] * points[1:2] + (points[2:3] * points[2:3] + offset)
    return split(total)


def kernel(
    slabs,
    geom_in,
    adj_in,
    str_in,
    tgt_in,
    own_in,
    src_in,
    ord_in,
    cnt_ref,
    corner_in,
    out_ref,
    geom_ref,
    adj_ref,
    str_ref,
    tgt_ref,
    own_ref,
    src_ref,
    ord_ref,
    corner_ref,
    load_sems,
    sgeom,
    sstr,
    tadj,
    tinfo,
    left,
    trow,
    sbase,
    srow,
    right,
    right_far,
    source_acc,
    target_acc,
    rs_source,
    rs_target,
    parts,
    landed,
    codes_v,
    codes,
    codes_sem,
    str_sems,
    geom_sems,
    send_sems,
    recv_sems,
):
    t, z, s, y, home = place(slabs)
    outer = slabs // FAR
    quarter = z // FAR
    tiles = slabs * SLAB
    mine = y == home
    other = jnp.logical_not(mine)
    barrier = pltpu.get_barrier_semaphore()
    near_first = {1: (0,), 2: (0, 1), 4: (0, 1, 3, 2)}[outer]
    near_last = {1: (0,), 2: (1, 0), 4: (1, 3, 2, 0)}[outer]
    shifts = (0, 1, tiles - 1, tiles // 2)

    loads = [
        pltpu.make_async_copy(src, dst, load_sems.at[n])
        for n, (src, dst) in enumerate(
            (
                (geom_in, geom_ref),
                (tgt_in, tgt_ref),
                (own_in, own_ref),
                (src_in, src_ref),
                (ord_in, ord_ref),
                (str_in, str_ref),
                (adj_in, adj_ref),
                (corner_in, corner_ref),
            )
        )
    ]
    def greet(device):
        pl.semaphore_signal(barrier, inc=1, device_id=device, device_id_type=MESH)

    for zz in range(outer):
        for dy in range(1, FAR):
            greet(((zz * FAR + y) * SLAB + s, (home + dy) % FAR))
    for dz in range(1, outer):
        greet(((((quarter + dz) % outer) * FAR + y) * SLAB + s, home))

    @pl.when(other)
    def _():
        greet(((quarter * FAR + y) * SLAB + s, home))

    for o in (3, 1, 2, 0):
        for dy in range(FAR):
            if o or dy:
                greet(((t + tiles - shifts[o]) % tiles, (y + dy) % FAR))
    for ds in range(1, SLAB):
        greet((z * SLAB + (s + ds) % SLAB, y))

    for load in loads:
        load.start()

    for load in loads:
        load.wait()

    lane = lax.broadcasted_iota(jnp.int32, (1, PB), 1)
    tinfo[s] = jnp.zeros((4, 4, PB), F32)
    for comp in range(3):
        for block in range(4):
            tinfo[s, block, comp : comp + 1, :] = geom_ref[comp, block : block + 1, :]
    live = lax.broadcasted_iota(jnp.int32, (1, PAIRS_DEV), 1) < cnt_ref[0]
    orders = jnp.where(live, ord_ref[...], 0)
    for row, values in enumerate((tgt_ref[...], own_ref[...], src_ref[...], orders)):
        tinfo[s, row, 3:4, 0:PAIRS_DEV] = values.astype(F32)

    pl.semaphore_wait(barrier, slabs - mine.astype(jnp.int32) + SLAB - 1 + 15)

    for dy in range(1, FAR):
        send(adj_ref, tadj.at[s, y], send_sems.at[2], recv_sems.at[2], (t, (y + dy) % FAR))
    tadj[s, y] = adj_ref[...]

    def send_strengths(zt):
        da = (quarter - zt // FAR + outer) % outer
        send(str_ref, sstr.at[da, y], send_sems.at[0], str_sems.at[da], (zt * SLAB + s, home))

    def send_geometry(zt):
        da = (quarter - zt // FAR + outer) % outer
        send(geom_ref, sgeom.at[da], send_sems.at[1], geom_sems.at[da], (zt * SLAB + s, home))

    for step in range(slabs // 2, 0, -1):
        send_strengths((z + step) % slabs)
        if 2 * step != slabs:
            send_strengths((z + slabs - step) % slabs)
    for dk in near_first[::-1]:
        if dk:
            send_geometry(((quarter + dk) % outer) * FAR + y)

    @pl.when(other)
    def _():
        send_strengths(z)
        send_geometry(quarter * FAR + y)

    @pl.when(mine)
    def _():
        sstr[0, y] = str_ref[...]
        sgeom[0] = geom_ref[...]

    for ds in range(1, SLAB):
        peer = (z * SLAB + (s + ds) % SLAB, y)
        send(tinfo.at[s], tinfo.at[s], send_sems.at[3], recv_sems.at[3], peer)
    wait(tadj.at[s, pl.ds(0, FAR - 1)], recv_sems.at[2])
    for ds in range(1, SLAB):
        peer = (z * SLAB + (s + ds) % SLAB, y)
        send(tadj.at[s], tadj.at[s], send_sems.at[4], recv_sems.at[4], peer)

    row = lax.broadcasted_iota(jnp.int32, (PB, PB), 0)
    picks = []
    keys = []
    for block in range(4):
        vertex = corner_ref[block]
        holder = vertex // (4 * PB)
        away = holder - t
        away = jnp.where(away < 0, away + tiles, away)
        group = jnp.where(
            away == 0, 0, jnp.where(away == 1, 1, jnp.where(away == tiles - 1, 2, 3))
        )
        within = vertex - holder * (4 * PB)
        high = within // PB
        low = within - high * PB
        keys.append(group * 4 + high)
        picks += [jnp.where(row == low[j : j + 1], 1.0, 0.0).astype(BF16) for j in range(4)]
    picks = jnp.concatenate(picks, axis=1)

    wait(tinfo.at[pl.ds(0, SLAB - 1)], recv_sems.at[3])
    place_of = lax.broadcasted_iota(jnp.int32, (8, PB), 0)
    wide_lane = lax.broadcasted_iota(jnp.int32, (8, PB), 1)
    da_of = place_of // 2
    wanted = ((quarter + da_of) % outer * FAR + y) * SLAB + s
    before = jnp.where(
        lax.broadcasted_iota(jnp.int32, (PB, PB), 0) < lax.broadcasted_iota(jnp.int32, (PB, PB), 1), 1.0, 0.0
    ).astype(BF16)
    for k in range(SLAB):
        target, owner, source, order = (tinfo[k, r, 3:4, :].astype(jnp.int32) for r in range(4))
        match = (owner == wanted) & (order > 0) & (wide_lane < PAIRS_DEV) & (da_of < outer)
        count = jnp.dot(
            jnp.where(match, 1.0, 0.0).astype(BF16), before, preferred_element_type=F32
        ).astype(jnp.int32)
        code = (target * 4 + source) * 4 + order
        chosen = jnp.where(match & (count == place_of - 2 * da_of), code, 0).astype(F32)
        total = jnp.sum(chosen, axis=1, keepdims=True).astype(jnp.int32)
        codes_v[k] = jnp.broadcast_to(total, (8, PB))
    copy = pltpu.make_async_copy(codes_v, codes, codes_sem)
    copy.start()

    wait(tadj.at[pl.ds(0, SLAB - 1)], recv_sems.at[4])
    zero4 = jnp.zeros((4, PB), F32)
    one = jnp.ones((1, PB), F32)
    zero1 = jnp.zeros((1, PB), F32)

    tile_row = lax.broadcasted_iota(jnp.int32, (4, PB), 0)

    def prepare_list(k, carry):
        conditions = [tadj[k, yy].astype(F32) for yy in range(FAR)]
        for block in range(4):
            centre = jnp.where(tile_row < 3, tinfo[k, block], 0.0)
            high, middle, low = split(centre)
            sq = squares(centre, 0.0)
            stack = jnp.concatenate(
                [c[4 * block : 4 * block + 4] for c in conditions]
                + [high, high, high, middle, middle, low]
                + [*sq, one, one, one, zero1, zero1],
                axis=0,
            )
            left[k * 4 + block] = stack.T.astype(BF16)
            trow[k * 4 + block] = jnp.concatenate(
                [one, zero1, zero1, zero1, high, middle, low], axis=0
            ).astype(BF16)
        target_acc[k] = jnp.zeros((4, 4, PB), F32)
        return carry

    lax.fori_loop(0, SLAB, prepare_list, 0)
    copy.wait()

    for da in near_last:
        if da:
            wait(sstr.at[da], str_sems.at[da])
            wait(sgeom.at[da], geom_sems.at[da])
        else:

            @pl.when(mine)
            def _():
                wait(sstr.at[0, pl.ds(0, FAR - 1)], str_sems.at[0])

            @pl.when(other)
            def _():
                wait(sstr.at[0], str_sems.at[0])
                wait(sgeom.at[0], geom_sems.at[0])

        conditions = [sstr[da, yy].astype(F32) for yy in range(FAR)]
        for block in range(4):
            base = jnp.concatenate([sgeom[da, c, block : block + 1, :] for c in range(3)] + [zero1], axis=0)
            half = 0.25 * jnp.concatenate(
                [sgeom[da, 3 + c, block : block + 1, :] for c in range(3)] + [zero1], axis=0
            )
            sbase[block] = jnp.concatenate([base, half], axis=0)
            first, second = split(base), split(half)
            srow[block] = jnp.concatenate(
                [
                    jnp.concatenate([one, zero1, zero1, zero1, *first], axis=0),
                    jnp.concatenate([zero4, *second], axis=0),
                ],
                axis=1,
            ).astype(BF16)

            def distance(points):
                high, middle, low = (-2.0 * part for part in split(points))
                sq = squares(points, 0.0625)
                return jnp.concatenate(
                    [zero4] * 4
                    + [high, middle, low, high, middle, high]
                    + [one, one, one, *sq, zero1, zero1],
                    axis=0,
                )

            coupled = jnp.concatenate(
                [c[4 * block : 4 * block + 4] for c in conditions] + [zero4] * 8, axis=0
            )
            right[block] = jnp.concatenate([coupled, distance(base)], axis=1).astype(BF16)
            for rule, node in enumerate((ROOT_HALF, ROOT_FIFTH)):
                right_far[block * 2 + rule] = jnp.concatenate(
                    [distance(base + node * half), distance(base - node * half)], axis=1
                ).astype(BF16)
        source_acc[da] = jnp.zeros((4, 4, PB), F32)

        def some_lists(group, carry, da=da):
            slots = []
            for step in range(GROUP):
                k = group * GROUP + step
                for occurrence in range(2):
                    code = codes[k, 2 * da + occurrence, 0]
                    slots.append((k, code & 3, (code >> 2) & 3, (code >> 4) & 3))
            products = []
            for k, order, source, target in slots:
                columns = left[k * 4 + target]
                products.append(
                    (
                        jnp.dot(columns, right[source], preferred_element_type=F32),
                        jnp.dot(
                            columns,
                            right_far[source * 2 + ((order + 1) >> 2)],
                            preferred_element_type=F32,
                        ),
                    )
                )
            factors = []
            for (k, order, source, target), (inner, sides) in zip(slots, products):
                centre_weight = jnp.where(order == 1, 1.0, jnp.where(order == 3, 4.0 / 9.0, 0.0))
                side_weight = jnp.where(order == 2, 0.5, jnp.where(order == 3, 5.0 / 18.0, 0.0))
                shift_weight = jnp.where(
                    order == 2, 0.5 * ROOT_HALF, jnp.where(order == 3, 5.0 / 18.0 * ROOT_FIFTH, 0.0)
                )
                roots = lax.rsqrt(inner[:, PB:])
                pulls = lax.rsqrt(sides)
                roots = roots * roots * roots
                pulls = pulls * pulls * pulls
                coupling = inner[:, :PB]
                plus, minus = pulls[:, :PB], pulls[:, PB:]
                both = coupling * (centre_weight * roots + side_weight * (plus + minus))
                skew = (shift_weight * coupling) * (plus - minus)
                high = jnp.concatenate([both.astype(BF16), skew.astype(BF16)], axis=1)
                low = jnp.concatenate(
                    [
                        (both - high[:, :PB].astype(F32)).astype(BF16),
                        (skew - high[:, PB:].astype(F32)).astype(BF16),
                    ],
                    axis=1,
                )
                factors.append((high, low))
            sums = []
            across = (((1,), (1,)), ((), ()))
            for (k, order, source, target), (high, low) in zip(slots, factors):
                rows, lines = trow[k * 4 + target], srow[source]
                sums.append(
                    (
                        jnp.dot(rows, high, preferred_element_type=F32)
                        + jnp.dot(rows, low, preferred_element_type=F32),
                        lax.dot_general(lines, high, across, preferred_element_type=F32)
                        + lax.dot_general(lines, low, across, preferred_element_type=F32),
                    )
                )
            gathered = [source_acc[da, block] for block in range(4)]
            returned = [None] * 4
            for n, ((k, order, source, target), (by_source, by_target)) in enumerate(zip(slots, sums)):
                points = sbase[source]
                pulled = (
                    by_source[4:8, :PB]
                    + by_source[8:12, :PB]
                    + by_source[12:16, :PB]
                    - points[0:4] * by_source[0:1, :PB]
                    - points[4:8] * by_source[0:1, PB:]
                )
                pushed = (
                    by_target[4:8]
                    + by_target[8:12]
                    + by_target[12:16]
                    - tinfo[k, target] * by_target[0:1]
                )
                for block in range(4):
                    gathered[block] = gathered[block] + jnp.where(source == block, 1.0, 0.0) * pulled
                    term = jnp.where(target == block, 1.0, 0.0) * pushed
                    returned[block] = term if n % 2 == 0 else returned[block] + term
                if n % 2:
                    for block in range(4):
                        target_acc[k, block] += returned[block]
            for block in range(4):
                source_acc[da, block] = gathered[block]
            return carry

        lax.fori_loop(0, SLAB // GROUP, some_lists, 0)

        def send_source(da=da):
            send(
                source_acc.at[da],
                rs_source.at[quarter],
                send_sems.at[5],
                recv_sems.at[5],
                ((((quarter + da) % outer) * FAR + y) * SLAB + s, home),
            )

        if da:
            send_source()
        else:
            pl.when(other)(send_source)

            @pl.when(mine)
            def _():
                rs_source[quarter] = source_acc[0]

    for ds in range(1, SLAB):
        st = (s + ds) % SLAB
        send(target_acc.at[st], rs_target.at[s], send_sems.at[6], recv_sems.at[6], (z * SLAB + st, y))
    rs_target[s] = target_acc[s]
    wait(rs_target.at[pl.ds(0, SLAB - 1)], recv_sems.at[6])

    @pl.when(mine)
    def _():
        if outer > 1:
            wait(rs_source.at[pl.ds(0, outer - 1)], recv_sems.at[5])

    @pl.when(other)
    def _():
        wait(rs_source.at[pl.ds(0, outer)], recv_sems.at[5])

    grad = jnp.sum(rs_target[...], axis=0) + jnp.sum(rs_source[...], axis=0)
    grad = grad * (0.25 * 0.0078125)
    rowkey = lax.broadcasted_iota(jnp.int32, (16, PB), 0)
    upper = [[], [], []]
    lower = [[], [], []]
    for block in range(4):
        for c in range(3):
            wide = jnp.broadcast_to(grad[block, c : c + 1], (16, PB))
            first = wide.astype(BF16)
            second = (wide - first.astype(F32)).astype(BF16)
            for j in range(4):
                here = rowkey == keys[block][j : j + 1]
                upper[c].append(jnp.where(here, first, jnp.zeros_like(first)))
                lower[c].append(jnp.where(here, second, jnp.zeros_like(second)))
    spread = jnp.concatenate([jnp.concatenate(part, axis=1) for part in upper + lower], axis=0)
    sums = lax.dot_general(spread, picks, (((1,), (1,)), ((), ())), preferred_element_type=F32)
    sums = sums[0:48] + sums[48:96]
    for o in range(4):
        for c in range(3):
            parts[o, c] = sums[16 * c + 4 * o : 16 * c + 4 * o + 4]
    for o in (3, 1, 2, 0):
        for dy in range(FAR):
            if o or dy:
                send(
                    parts.at[o],
                    landed.at[o * FAR + dy],
                    send_sems.at[7],
                    recv_sems.at[7],
                    ((t + shifts[o]) % tiles, (y + dy) % FAR),
                )
    landed[0] = parts[0]
    wait(landed.at[pl.ds(1, 15)], recv_sems.at[7])
    result = jnp.sum(landed[...], axis=0)
    for k in range(4):
        for c in range(3):
            out_ref[c : c + 1, k * PB : (k + 1) * PB] = result[c, k : k + 1]

    wait(tadj.at[s, pl.ds(0, FAR - 1)], send_sems.at[2])
    wait(tinfo.at[pl.ds(0, SLAB - 1)], send_sems.at[3])
    wait(tadj.at[pl.ds(0, SLAB - 1)], send_sems.at[4])
    wait(rs_target.at[pl.ds(0, SLAB - 1)], send_sems.at[6])
    wait(landed.at[pl.ds(1, 15)], send_sems.at[7])

    @pl.when(mine)
    def _():
        if outer > 1:
            wait(sstr.at[pl.ds(0, outer - 1)], send_sems.at[0])
            wait(sgeom.at[pl.ds(0, outer - 1)], send_sems.at[1])
            wait(rs_source.at[pl.ds(0, outer - 1)], send_sems.at[5])
        wait(sstr.at[0, pl.ds(0, FAR - 1)], send_sems.at[0])

    @pl.when(other)
    def _():
        wait(sstr, send_sems.at[0])
        wait(sgeom, send_sems.at[1])
        wait(rs_source, send_sems.at[5])


def resident(dims, dtype):
    return pltpu.VMEM(dims, dtype)


def vmem():
    return pl.BlockSpec(memory_space=pltpu.VMEM)


def anywhere():
    return pl.BlockSpec(memory_space=pl.ANY)


def smem():
    return pl.BlockSpec(memory_space=pltpu.SMEM)


def per_device(
    panel_geometry,
    adjoint,
    strengths,
    pair_target,
    pair_owner,
    pair_source,
    pair_order,
    pair_count,
    corner_vertex,
):
    slabs = lax.axis_size("tiles") // SLAB
    outer = slabs // FAR
    row = lambda values: values.reshape(1, PAIRS_DEV)
    return pl.pallas_call(
        functools.partial(kernel, slabs),
        out_shape=resident((3, WITHIN), F32),
        in_specs=[anywhere()] * 7 + [smem(), anywhere()],
        out_specs=vmem(),
        scratch_shapes=[
            pltpu.VMEM((6, 4, PB), F32),
            pltpu.VMEM((16, PB), BF16),
            pltpu.VMEM((16, PB), BF16),
            pltpu.VMEM((1, PAIRS_DEV), jnp.int32),
            pltpu.VMEM((1, PAIRS_DEV), jnp.int32),
            pltpu.VMEM((1, PAIRS_DEV), jnp.int32),
            pltpu.VMEM((1, PAIRS_DEV), jnp.int32),
            pltpu.VMEM((4, 4, PB), jnp.int32),
            pltpu.SemaphoreType.DMA((8,)),
            pltpu.VMEM((outer, 6, 4, PB), F32),
            pltpu.VMEM((outer, FAR, 16, PB), BF16),
            pltpu.VMEM((SLAB, FAR, 16, PB), BF16),
            pltpu.VMEM((SLAB, 4, 4, PB), F32),
            pltpu.VMEM((SLAB * 4, PB, 48), BF16),
            pltpu.VMEM((SLAB * 4, 16, PB), BF16),
            pltpu.VMEM((4, 8, PB), F32),
            pltpu.VMEM((4, 16, 2 * PB), BF16),
            pltpu.VMEM((4, 48, 2 * PB), BF16),
            pltpu.VMEM((8, 48, 2 * PB), BF16),
            pltpu.VMEM((outer, 4, 4, PB), F32),
            pltpu.VMEM((SLAB, 4, 4, PB), F32),
            pltpu.VMEM((outer, 4, 4, PB), F32),
            pltpu.VMEM((SLAB, 4, 4, PB), F32),
            pltpu.VMEM((4, 3, 4, PB), F32),
            pltpu.VMEM((16, 3, 4, PB), F32),
            pltpu.VMEM((SLAB, 8, PB), jnp.int32),
            pltpu.SMEM((SLAB, 8, PB), jnp.int32),
            pltpu.SemaphoreType.DMA,
            pltpu.SemaphoreType.DMA((outer,)),
            pltpu.SemaphoreType.DMA((outer,)),
            pltpu.SemaphoreType.DMA((8,)),
            pltpu.SemaphoreType.DMA((8,)),
        ],
        compiler_params=pltpu.CompilerParams(
            collective_id=0, has_side_effects=True
        ),
        name="gather_pairs_return",
    )(
        panel_geometry.transpose(1, 0, 2),
        adjoint.reshape(16, PB),
        strengths.reshape(16, PB),
        row(pair_target),
        row(pair_owner),
        row(pair_source),
        row(pair_order),
        pair_count,
        corner_vertex,
    )


def solution(mesh):
    placed = (
        P("tiles", None, None),
        P("tiles", "far", None),
        P("tiles", "far", None),
        P("tiles"),
        P("tiles", None),
        P("tiles"),
        P("tiles"),
        P("tiles"),
        P("tiles", None, None),
    )
    return jax.shard_map(
        per_device, mesh=mesh, in_specs=placed, out_specs=P(None, "tiles"), check_vma=False
    )
```
